256 devices in a mesh: gx: 32 (over z, x), gy: 8 (over y, core).
Axes of the slice: x: 4, y: 4, z: 8, core: 2. Of those that a mesh axis runs over, the one named last changes fastest.
Arguments:
- features: bfloat16 [65536, 128], P(('gx', 'gy')), may hold values from -6 to 6
- edge_vec: float32 [3, 1048576], P(None, ('gx', 'gy')), may hold values from -6 to 6
- edge_src: int32 [1048576], P(('gx', 'gy')), may hold values from 0 to 1407
- edge_dst: int32 [1048576], P(('gx', 'gy')), may hold values from 0 to 255
- edge_count: int32 [256], P(('gx', 'gy')), may hold values from 1024 to 4096
- send_gx: int32 [1024, 192], P(('gx', 'gy')), may hold values from 0 to 255
- send_gy: int32 [512, 192], P(('gx', 'gy')), may hold values from 0 to 255
- w_one: float32 [8, 64], replicated, may hold values from -2 to 2
- w_two: float32 [64, 384], replicated, may hold values from -0.75 to 0.75
- mix: float32 [3, 128, 128], replicated, may hold values from -0.5 to 0.5
- cotangent: bfloat16 [65536, 1152], P(('gx', 'gy')), may hold values from -6 to 6
Outputs:
- mixed: bfloat16 [65536, 1152], P(('gx', 'gy'))
- grad_features: float32 [65536, 128], P(('gx', 'gy'))
- edge_force: float32 [3, 1048576], P(None, ('gx', 'gy'))
- grad_w_one: float32 [8, 64], replicated
- grad_w_two: float32 [64, 384], replicated
- grad_mix: float32 [3, 128, 128], replicated
The draws below stay inside these ranges and needn't reach their ends.
Inputs may be any that keep to these rules, and one draw needn't show every extreme that they name: `edge_src`: a row of a tile's table. `edge_dst`: an owned atom of the tile. `send_gx`: an owned atom of the sending tile. `send_gy`: an owned atom of the sending tile.
All inputs are finite; a program needn't handle non-finite values.
Results may differ from the reference program's by a relative error of at most 0.006.
Values may be sent and summed in bfloat16 or wider, within the bound.
A program may use at most 192 MiB of HBM per device.

```python
import math
import jax
import jax.numpy as jnp
from jax import lax

C = 128
HID = 64
BASIS = 8
A_DEV = 256
S_PEER = 192
E_DEV = 4096
TABLE = 1408
ATOMS = 65536
EDGES = 1048576
N_GX = 32
N_GY = 8
DEVICES = 256


def with_ends(drawn, key, smallest, largest):
    longest = drawn.shape.index(max(drawn.shape))
    spots = []
    for shift in (0, 1):
        where = [jax.random.randint(jax.random.fold_in(key, axis), (), 0, length) for axis, length in enumerate(drawn.shape)]
        where[longest] = (where[longest] + shift) % drawn.shape[longest]
        spots.append(tuple(where))
    return drawn.at[spots[0]].set(smallest).at[spots[1]].set(largest)


def levels(stream_key, extent, split, least, high):
    loudness = 1.0
    for dim, parts in split:
        draws = jax.random.uniform(jax.random.fold_in(jax.random.fold_in(stream_key, 6), dim), (parts,), jnp.float32, least / len(split), high / len(split))
        loudness = loudness * jnp.repeat(jnp.exp(draws), extent[dim] // parts).reshape((-1,) + (1,) * (len(extent) - 1 - dim))
    return loudness


def normal_values(own_key, extent, scale, limit, pieces=(), held_as=jnp.bfloat16):
    factor_of = levels(own_key, extent, pieces, -0.22, 0.18) if pieces else 1.0
    drawn = jax.random.normal(own_key, extent, jnp.float32) * scale * factor_of
    return jnp.minimum(jnp.maximum(drawn, -limit), limit).astype(held_as)


def setup_inputs(seed: int = 0) -> dict:
    arg_keys = jax.random.split(jax.random.key(seed), 12)
    return {
        "features": normal_values(arg_keys[0], (ATOMS, C), 1.0, 6.0, ((0, 256),)),
        "edge_vec": normal_values(arg_keys[1], (3, EDGES), 1.5, 6.0, ((1, 256),), jnp.float32),
        "edge_src": with_ends(jax.random.randint(arg_keys[2], (EDGES,), 0, TABLE), jax.random.fold_in(arg_keys[2], 1), 0, TABLE - 1).astype(jnp.int32),
        "edge_dst": with_ends(jax.random.randint(arg_keys[3], (EDGES,), 0, A_DEV), jax.random.fold_in(arg_keys[3], 1), 0, A_DEV - 1).astype(jnp.int32),
        "edge_count": with_ends(jax.random.randint(arg_keys[4], (DEVICES,), E_DEV // 4, E_DEV + 1), jax.random.fold_in(arg_keys[4], 1), E_DEV // 4, E_DEV).astype(jnp.int32),
        "send_gx": with_ends(jax.random.randint(arg_keys[5], (DEVICES * 4, S_PEER), 0, A_DEV), jax.random.fold_in(arg_keys[5], 1), 0, A_DEV - 1).astype(jnp.int32),
        "send_gy": with_ends(jax.random.randint(arg_keys[6], (DEVICES * 2, S_PEER), 0, A_DEV), jax.random.fold_in(arg_keys[6], 1), 0, A_DEV - 1).astype(jnp.int32),
        "w_one": normal_values(arg_keys[7], (BASIS, HID), BASIS ** -0.5, 2.0, (), jnp.float32),
        "w_two": normal_values(arg_keys[8], (HID, 3 * C), HID ** -0.5, 0.75, (), jnp.float32),
        "mix": normal_values(arg_keys[9], (3, C, C), C ** -0.5, 0.5, (), jnp.float32),
        "cotangent": normal_values(arg_keys[10], (ATOMS, 9 * C), 1.0, 6.0, ((0, 256),)),
    }


DEGREE = [0, 1, 1, 1, 2, 2, 2, 2, 2]

def harmonics(unit):
    xval, yval, zval = (unit[0], unit[1], unit[2])
    root_three = math.sqrt(3.0)
    root_fifteen = math.sqrt(15.0)
    return [jnp.ones_like(xval), root_three * xval, root_three * yval, root_three * zval, root_fifteen * xval * yval, root_fifteen * yval * zval, 0.5 * math.sqrt(5.0) * (3.0 * zval * zval - 1.0), root_fifteen * xval * zval, 0.5 * root_fifteen * (xval * xval - yval * yval)]

def interaction(table, vec, w_one, w_two, mix, src, dst, live, owned):
    hp = lax.Precision.HIGHEST
    dist = jnp.sqrt(lax.optimization_barrier(jnp.sum(vec * vec, axis=0)) + 0.25)
    unit = vec / dist
    ratio = dist / 5.0
    freq = jnp.arange(1, w_one.shape[0] + 1).astype(jnp.float32)
    basis = jnp.sin(freq[:, None] * math.pi * ratio[None, :]) / dist / (1.0 + ratio ** 6)
    hidden = jax.nn.silu(jnp.dot(w_one.T, basis, precision=hp))
    radial = jnp.dot(w_two.T, hidden, precision=hp) * live
    edges = vec.shape[1]
    width = table.shape[1]
    radial_rows = radial.T.reshape(edges, 3, width)
    gathered = table[src]
    factor = math.sqrt(owned / edges)
    harm = harmonics(unit)
    weighted = [radial_rows[:, 0] * gathered, radial_rows[:, 1] * gathered, radial_rows[:, 2] * gathered]
    sums = []
    for comp in range(9):
        term = weighted[DEGREE[comp]] * (harm[comp] * factor)[:, None]
        sums.append(jax.ops.segment_sum(term, dst, num_segments=owned))
    acc = jnp.stack(sums, axis=1)
    outs = [jnp.einsum('amc,cd->amd', acc[:, 0:1], mix[0], precision=hp), jnp.einsum('amc,cd->amd', acc[:, 1:4], mix[1], precision=hp), jnp.einsum('amc,cd->amd', acc[:, 4:9], mix[2], precision=hp)]
    return jnp.concatenate(outs, axis=1).reshape(owned, 9 * width)

def reference(features, edge_vec, edge_src, edge_dst, edge_count, send_gx, send_gy, w_one, w_two, mix, cotangent):
    n_dev = N_GX * N_GY
    owned = A_DEV
    edges = E_DEV
    row_lists = send_gx.reshape(n_dev, 4, S_PEER)
    col_lists = send_gy.reshape(n_dev, 2, S_PEER)
    vec_dev = edge_vec.reshape(3, n_dev, edges)
    steps_x = jnp.array([1, -1, 2, -2], dtype=jnp.int32)
    steps_y = jnp.array([1, -1], dtype=jnp.int32)

    def one_tile(dev):
        gxi = dev // N_GY
        gyj = dev % N_GY
        peers_x = ((gxi - steps_x) % N_GX * N_GY + gyj).astype(jnp.int32)
        ghost_x = row_lists[peers_x, jnp.arange(4).astype(jnp.int32)] + peers_x[:, None] * owned
        peers_y = (gxi * N_GY + (gyj - steps_y) % N_GY).astype(jnp.int32)
        ghost_y = col_lists[peers_y, jnp.arange(2).astype(jnp.int32)] + peers_y[:, None] * owned
        own_rows = dev * owned + jnp.arange(owned).astype(jnp.int32)
        rows = jnp.concatenate([own_rows, ghost_x.reshape(-1).astype(jnp.int32), ghost_y.reshape(-1).astype(jnp.int32)]).astype(jnp.int32)
        table = features[rows].astype(jnp.float32)
        vec = vec_dev[:, dev]
        src = lax.dynamic_slice_in_dim(edge_src, dev * edges, edges)
        dst = lax.dynamic_slice_in_dim(edge_dst, dev * edges, edges)
        live = (jnp.arange(edges).astype(jnp.int32) < edge_count[dev]).astype(jnp.float32)
        grad_out = lax.dynamic_slice_in_dim(cotangent, dev * owned, owned).astype(jnp.float32)

        def local(tab, vv, wa, wb, mm):
            return interaction(tab, vv, wa, wb, mm, src, dst, live, owned)
        out, pull = jax.vjp(local, table, vec, w_one, w_two, mix)
        d_table, d_vec, d_one, d_two, d_mix = pull(grad_out)
        return (out.astype(jnp.bfloat16), d_table, d_vec, d_one, d_two, d_mix, rows)
    outs = lax.map(one_tile, jnp.arange(n_dev).astype(jnp.int32))
    mixed = outs[0].reshape(n_dev * owned, 9 * C)
    grad_features = jax.ops.segment_sum(outs[1].reshape(-1, C), outs[6].reshape(-1), num_segments=n_dev * owned)
    edge_force = jnp.transpose(outs[2], (1, 0, 2)).reshape(3, n_dev * edges)
    return (mixed, grad_features, edge_force, lax.optimization_barrier(jnp.sum(outs[3], axis=0)), lax.optimization_barrier(jnp.sum(outs[4], axis=0)), lax.optimization_barrier(jnp.sum(outs[5], axis=0)))
```

```python
import functools
import math

import jax
import jax.numpy as jnp
from jax import lax
from jax.experimental import pallas as pl
from jax.experimental.pallas import tpu as pltpu
from jax.sharding import PartitionSpec as P

F32 = jnp.float32
BF16 = jnp.bfloat16
DEGREE = [0, 1, 1, 1, 2, 2, 2, 2, 2]
ROW_STEPS = [1, -1, 2, -2]
COLUMN_STEPS = [1, -1]
CHUNK = 256
SLICE = 80
PIECE = 8


def mm(a, b):
    return jnp.dot(a, b, preferred_element_type=F32)


def mm_nt(a, b):
    return lax.dot_general(a, b, (((1,), (1,)), ((), ())), preferred_element_type=F32)


def eye(n):
    rows = lax.broadcasted_iota(jnp.int32, (n, n), 0)
    cols = lax.broadcasted_iota(jnp.int32, (n, n), 1)
    return jnp.where(rows == cols, 1.0, 0.0).astype(BF16)


def split(a):
    hi = a.astype(BF16)
    lo = (a - hi.astype(F32)).astype(BF16)
    return hi, lo


def kernel(
    nx,
    ny,
    block,
    features,
    vec,
    src,
    dst,
    count,
    send_x,
    send_y,
    w_one,
    w_two,
    mix,
    cot,
    mixed,
    grad_feat,
    force,
    grad_one,
    grad_two,
    grad_mix,
    table,
    outgoing,
    dtab_out,
    back,
    dtab,
    acc,
    dacc,
    one_src,
    one_dst,
    radial,
    dweight,
    dterms,
    dsilu,
    hidden,
    harm,
    basis2,
    dbasis,
    geom,
    part,
    dharm,
    ddist,
    dw_two,
    dw_one,
    ar,
    ar_half,
    got_one,
    red_one,
    got_two,
    red_two,
    red_three,
    half_three,
    final,
    ghost_send,
    ghost_recv,
    back_send,
    back_recv,
    one_send,
    one_recv,
    two_send,
    two_recv,
    three_send,
    three_recv,
    four_send,
    four_recv,
):
    owned, width = features.shape
    edges = vec.shape[1]
    slots = send_x.shape[1]
    comm = nx > 1
    chunks = table.shape[0] // CHUNK
    me_x = lax.axis_index("gx")
    me_y = lax.axis_index("gy")
    factor = math.sqrt(owned / edges)

    if comm:
        barrier = pltpu.get_barrier_semaphore()

        def greet_x(s, c):
            pl.semaphore_signal(
                barrier, inc=1, device_id={"gx": lax.rem(me_x + s, nx)}, device_id_type=pl.DeviceIdType.MESH
            )
            return c

        def greet_y(s, c):
            pl.semaphore_signal(
                barrier, inc=1, device_id={"gy": lax.rem(me_y + s, ny)}, device_id_type=pl.DeviceIdType.MESH
            )
            return c

        lax.fori_loop(1, ny, greet_y, 0)
        lax.fori_loop(1, nx, greet_x, 0)

    def to_peer(p, source, target, sends, recvs, sign):
        if p < 4:
            where = {"gx": lax.rem(me_x + sign * ROW_STEPS[p] + nx, nx)}
        else:
            where = {"gy": lax.rem(me_y + sign * COLUMN_STEPS[p - 4] + ny, ny)}
        if not comm:
            return pltpu.make_async_copy(source, target, recvs.at[p])
        return pltpu.make_async_remote_copy(
            src_ref=source,
            dst_ref=target,
            send_sem=sends.at[p],
            recv_sem=recvs.at[p],
            device_id=where,
            device_id_type=pl.DeviceIdType.MESH,
        )

    eye256 = eye(256)
    eye128 = eye256[:128, :128]
    feats = features[...]

    def picks(p):
        row = send_x[p : p + 1, :] if p < 4 else send_y[p - 4 : p - 3, :]
        rows = lax.broadcasted_iota(jnp.int32, (owned, slots), 0)
        return jnp.where(rows == row, 1.0, 0.0).astype(BF16)

    eye_slots = eye256[:slots, :slots]
    for p in range(6):
        pick = mm_nt(eye_slots, picks(p)).astype(BF16)
        outgoing[p * slots : (p + 1) * slots, :] = mm(pick, feats).astype(BF16)
    if comm:
        pl.semaphore_wait(barrier, nx + ny - 2)
    ghosts = [
        to_peer(
            p,
            outgoing.at[pl.ds(p * slots, slots)],
            table.at[pl.ds(owned + p * slots, slots)],
            ghost_send,
            ghost_recv,
            1,
        )
        for p in range(6)
    ]
    for copy in ghosts:
        copy.start()

    table[0:owned, :] = feats
    used = owned + 6 * slots
    table[used:, :] = jnp.zeros((table.shape[0] - used, width), BF16)
    dtab[...] = jnp.zeros_like(dtab)
    acc[...] = jnp.zeros_like(acc)
    dw_two[...] = jnp.zeros_like(dw_two)
    dw_one[...] = jnp.zeros_like(dw_one)

    w1h, w1l = split(w_one[...])
    w1h = w1h.astype(F32)
    w1l = w1l.astype(F32)
    w1_both = jnp.concatenate([w1h, w1l], axis=0).astype(BF16)
    w1_stack = jnp.concatenate([w1h, w1h, w1l, jnp.zeros_like(w1l)], axis=0).astype(BF16)
    w1_t = mm_nt(eye256[:64, :64], w1_stack).astype(BF16)
    w2h, w2l = split(w_two[...])
    w2_both = jnp.concatenate([w2h, w2l], axis=0)
    w2_stack = jnp.concatenate([w2h, w2h, w2l], axis=0)
    w2_t = [
        mm_nt(eye128, w2_stack[:, deg * width : (deg + 1) * width]).astype(BF16) for deg in range(3)
    ]
    mix_hl = []
    for deg in range(3):
        hi, lo = split(mix[deg])
        mix_hl.append((hi, lo))
    for m in range(9):
        hi, lo = mix_hl[DEGREE[m]]
        cot_m = cot[:, m * width : (m + 1) * width]
        both = mm_nt(jnp.concatenate([hi, lo], axis=1), jnp.concatenate([cot_m, cot_m], axis=1))
        dacc[m * width : (m + 1) * width, :] = (both * factor).astype(BF16)

    live_count = count[0]
    r3 = math.sqrt(3.0)
    r5 = math.sqrt(5.0)
    r15 = math.sqrt(15.0)
    pi = math.pi

    def part_one(b, carry):
        start = pl.multiple_of(b * block, block)
        sl = pl.ds(start, block)
        v = vec[:, sl]
        x, y, z = v[0:1], v[1:2], v[2:3]
        dist = jnp.sqrt(x * x + y * y + z * z + 0.25)
        inv = 1.0 / dist
        ratio = dist * (1.0 / 5.0)
        ra2 = ratio * ratio
        ra5 = ra2 * ra2 * ratio
        env = 1.0 / (1.0 + ra5 * ratio)
        ux, uy, uz = x * inv, y * inv, z * inv
        geom[0:1, sl] = ux
        geom[1:2, sl] = uy
        geom[2:3, sl] = uz
        geom[3:4, sl] = inv
        hs = [
            r3 * ux,
            r3 * uy,
            r3 * uz,
            r15 * ux * uy,
            r15 * uy * uz,
            0.5 * r5 * (3.0 * uz * uz - 1.0),
            r15 * ux * uz,
            0.5 * r15 * (ux * ux - uy * uy),
        ]
        for i in range(8):
            harm[i : i + 1, sl] = hs[i]
        k = (lax.broadcasted_iota(jnp.int32, (8, block), 0) + 1).astype(F32)
        t = k * ratio
        n = jnp.floor(t + 0.5)
        r = t - n
        sgn = 1.0 - 2.0 * (n - 2.0 * jnp.floor(n * 0.5))
        q = r * r
        s_pi = pi**9 / 362880.0 - q * (pi**11 / 39916800.0)
        s_pi = pi**7 / 5040.0 - q * s_pi
        s_pi = pi**5 / 120.0 - q * s_pi
        s_pi = pi**3 / 6.0 - q * s_pi
        s_pi = r * (pi - q * s_pi)
        c_pi = pi**10 / 3628800.0 - q * (pi**12 / 479001600.0)
        c_pi = pi**8 / 40320.0 - q * c_pi
        c_pi = pi**6 / 720.0 - q * c_pi
        c_pi = pi**4 / 24.0 - q * c_pi
        c_pi = pi**2 / 2.0 - q * c_pi
        c_pi = 1.0 - q * c_pi
        amp = sgn * (inv * env)
        bas = s_pi * amp
        dbasis[:, sl] = c_pi * amp * (k * (pi / 5.0)) - bas * (inv + (6.0 / 5.0) * (env * ra5))
        bh = bas.astype(BF16).astype(F32)
        bl = bas - bh
        basis2[:, sl] = jnp.concatenate([bh, bl], axis=0).astype(BF16)
        bstack = jnp.concatenate([bh, bl, bh, jnp.zeros_like(bh)], axis=0).astype(BF16)
        pre = mm(w1_t, bstack)
        spot = lax.broadcasted_iota(jnp.int32, (1, block), 1) + start
        live = jnp.where(spot < live_count, 1.0, 0.0)
        sig = 1.0 / (1.0 + jnp.exp(-pre))
        sig_live = sig * live
        hid = pre * sig_live
        dsilu[:, sl] = sig_live * (1.0 + pre * (1.0 - sig))
        hh, hl = split(hid)
        hidden[:, sl] = hh
        hstack = jnp.concatenate([hh, hl, hh], axis=0)
        for deg in range(3):
            radial[deg * width : (deg + 1) * width, sl] = mm(w2_t[deg], hstack)
        index = src[:, sl]
        chunk = lax.shift_right_logical(index, 8)
        part[:, sl] = chunk
        rows = lax.broadcasted_iota(jnp.int32, (CHUNK, block), 0)
        one_src[:, sl] = jnp.where(rows == index - chunk * CHUNK, 1.0, 0.0).astype(BF16)
        pick = jnp.where(rows == dst[:, sl], 1.0, 0.0).astype(BF16)
        one_dst[:, sl] = pick
        total = None
        for m in range(9):
            rws = slice(m * width, (m + 1) * width)
            term = mm(dacc[rws, :], pick)
            dterms[rws, sl] = term
            if m > 0:
                term = term * hs[m - 1]
            total = term if total is None else total + term
            if m in (0, 3, 8):
                deg = DEGREE[m]
                dweight[deg * width : (deg + 1) * width, sl] = total
                total = None
        return carry

    lax.fori_loop(0, edges // block, part_one, 0)

    for copy in ghosts:
        if comm:
            copy.wait_recv()
        else:
            copy.wait()
    table_t = jnp.concatenate(
        [mm_nt(eye128, table[c * CHUNK : (c + 1) * CHUNK, :]).astype(BF16) for c in range(chunks)], axis=0
    )

    def part_two(b, carry):
        start = pl.multiple_of(b * block, block)
        sl = pl.ds(start, block)
        ones = one_src[:, sl]
        chunk = part[:, sl]
        got = mm(table_t, ones)
        g = got[0:width]
        for c in range(1, chunks):
            g = jnp.where(chunk == c, got[c * width : (c + 1) * width], g)
        rad = [radial[deg * width : (deg + 1) * width, sl] for deg in range(3)]
        dwt = [dweight[deg * width : (deg + 1) * width, sl] for deg in range(3)]
        dg = rad[0] * dwt[0] + rad[1] * dwt[1] + rad[2] * dwt[2]
        dgm = jnp.concatenate([jnp.where(chunk == c, dg, 0.0).astype(BF16) for c in range(chunks)], axis=0)
        dtab[...] += mm_nt(ones, dgm)
        drad = jnp.concatenate([(dwt[deg] * g).astype(BF16) for deg in range(3)], axis=0)
        dhid = mm(w2_both, drad)
        dpre = ((dhid[:64] + dhid[64:]) * dsilu[:, sl]).astype(BF16)
        dw_two[...] += mm_nt(hidden[:, sl], drad)
        dw_one[...] += mm_nt(basis2[:, sl], dpre)
        dbas = mm(w1_both, dpre)
        ddist[:, sl] = jnp.sum((dbas[:8] + dbas[8:]) * dbasis[:, sl], axis=0, keepdims=True)
        pick = one_dst[:, sl]
        weighted = [rad[deg] * g for deg in range(3)]
        for m in range(9):
            rws = slice(m * width, (m + 1) * width)
            w = weighted[DEGREE[m]]
            if m == 0:
                term = w
            else:
                term = w * harm[m - 1 : m, sl]
                dharm[m - 1 : m, sl] = jnp.sum(w * dterms[rws, sl], axis=0, keepdims=True)
            acc[rws, :] += mm_nt(term.astype(BF16), pick)
        return carry

    lax.fori_loop(0, edges // block, part_two, 0)

    for c in range(chunks):
        dtab_out[c * CHUNK : (c + 1) * CHUNK, :] = dtab[:, c * width : (c + 1) * width].astype(BF16)
    returns = [
        to_peer(
            p,
            dtab_out.at[pl.ds(owned + p * slots, slots)],
            back.at[pl.ds(p * slots, slots)],
            back_send,
            back_recv,
            -1,
        )
        for p in range(6)
    ]
    for copy in returns:
        copy.start()

    accb = [(acc[m * width : (m + 1) * width, :] * factor).astype(BF16) for m in range(9)]
    for deg in range(3):
        total = None
        for m in range(9):
            if DEGREE[m] == deg:
                one = mm(accb[m], cot[:, m * width : (m + 1) * width])
                total = one if total is None else total + one
        ar[deg * width : (deg + 1) * width, :] = total
    row = 3 * width
    for deg in range(3):
        ar[row : row + 64, :] = dw_two[:, deg * width : (deg + 1) * width]
        row += 64
    ar[row:, :] = jnp.zeros((ar.shape[0] - row, width), F32)
    ar[row : row + 8, 0:64] = dw_one[0:8, :] + dw_one[8:16, :]
    row_one = row

    def mesh_copy(axis, index, source, target, send, recv):
        return pltpu.make_async_remote_copy(
            src_ref=source,
            dst_ref=target,
            send_sem=send,
            recv_sem=recv,
            device_id={axis: index},
            device_id_type=pl.DeviceIdType.MESH,
        )

    def rows_of(q):
        return pl.ds(pl.multiple_of(q * SLICE, 16), SLICE)

    pieces = SLICE // PIECE
    stride = nx // pieces

    def copy_one(s):
        q = lax.rem(me_y + s, ny)
        return mesh_copy("gy", q, ar_half.at[rows_of(q)], got_one.at[s], one_send.at[s], one_recv.at[s])

    def copy_two(t):
        return mesh_copy(
            "gx",
            t * stride,
            red_one.at[pl.ds(pl.multiple_of(t * PIECE, PIECE), PIECE)],
            got_two.at[me_x],
            two_send.at[t],
            two_recv.at[me_x],
        )

    def from_two(s):
        return mesh_copy("gx", s, red_two, got_two.at[s], two_send.at[0], two_recv.at[s])

    def copy_three(s, t):
        return mesh_copy(
            "gx",
            lax.rem(me_x + s, nx),
            red_two,
            red_three.at[pl.ds(pl.multiple_of(t * PIECE, PIECE), PIECE)],
            three_send.at[s],
            three_recv.at[t],
        )

    def copy_four(s):
        q = lax.rem(me_y + s, ny)
        return mesh_copy("gy", q, half_three, final.at[rows_of(me_y)], four_send.at[s], four_recv.at[s])

    def from_four(s):
        q = lax.rem(me_y + ny - s, ny)
        return mesh_copy("gy", q, half_three, final.at[rows_of(q)], four_send.at[s], four_recv.at[s])

    def loop(low, high, f):
        def step(s, c):
            f(s)
            return c

        lax.fori_loop(low, high, step, 0)

    my_piece = lax.div(me_x, stride)
    owner = jnp.logical_and(lax.rem(me_x, stride) == 0, my_piece < pieces)

    if comm:
        ar_half[...] = ar[...].astype(BF16)
        loop(1, ny, lambda s: copy_one(s).start())

    for m in range(9):
        hi, lo = mix_hl[DEGREE[m]]
        mix_t = jnp.concatenate([mm_nt(eye128, hi), mm_nt(eye128, lo)], axis=1).astype(BF16)
        out_t = mm(mix_t, jnp.concatenate([accb[m], accb[m]], axis=0)).astype(BF16)
        mixed[:, m * width : (m + 1) * width] = mm_nt(eye256, out_t).astype(BF16)

    if comm:
        red_one[...] = ar[rows_of(me_y), :]

        def add_one(s):
            copy_one(s).wait_recv()
            red_one[...] += got_one[s].astype(F32)

        loop(1, ny, add_one)

        def send_two(t):
            @pl.when(me_x != t * stride)
            def _():
                copy_two(t).start()

        loop(0, pieces, send_two)

    ux, uy, uz, inv = (geom[i : i + 1, :] for i in range(4))
    g1, g2, g3, g4, g5, g6, g7, g8 = (dharm[i : i + 1, :] for i in range(8))
    dx = r3 * g1 + r15 * (g4 * uy + g7 * uz + g8 * ux)
    dy = r3 * g2 + r15 * (g4 * ux + g5 * uz - g8 * uy)
    dz = r3 * g3 + r15 * (g5 * uy + g7 * ux) + (3.0 * r5) * (uz * g6)
    dd = ddist[...] - (dx * ux + dy * uy + dz * uz) * inv
    force[0:1, :] = dx * inv + ux * dd
    force[1:2, :] = dy * inv + uy * dd
    force[2:3, :] = dz * inv + uz * dd

    if comm:

        @pl.when(owner)
        def _():
            red_two[...] = red_one[pl.ds(pl.multiple_of(my_piece * PIECE, PIECE), PIECE), :]

            def add_two(s):
                @pl.when(s != me_x)
                def _():
                    from_two(s).wait_recv()
                    red_two[...] += got_two[s]

            loop(0, nx, add_two)
            loop(1, nx, lambda s: copy_three(s, my_piece).start())
            red_three[pl.ds(pl.multiple_of(my_piece * PIECE, PIECE), PIECE), :] = red_two[...]

    for copy in returns:
        if comm:
            copy.wait_recv()
        else:
            copy.wait()
    total = dtab[:, 0:width]
    for p in range(6):
        total = total + mm(picks(p), back[p * slots : (p + 1) * slots, :])
    grad_feat[...] = total

    if comm:

        def wait_three(t):
            @pl.when(me_x != t * stride)
            def _():
                copy_three(0, t).wait_recv()

        loop(0, pieces, wait_three)
        half_three[...] = red_three[...].astype(BF16)
        loop(1, ny, lambda s: copy_four(s).start())
        final[rows_of(me_y), :] = half_three[...]
        loop(1, ny, lambda s: from_four(s).wait_recv())
        last = final
    else:
        last = ar
    for deg in range(3):
        grad_mix[deg] = last[deg * width : (deg + 1) * width, :].astype(F32)
    row = 3 * width
    for deg in range(3):
        grad_two[:, deg * width : (deg + 1) * width] = last[row : row + 64, :].astype(F32)
        row += 64
    grad_one[...] = last[row_one : row_one + 16, :].astype(F32)[0:8, 0:64]

    if comm:
        for copy in ghosts:
            copy.wait_send()
        for copy in returns:
            copy.wait_send()
        loop(1, ny, lambda s: copy_one(s).wait_send())

        def end_two(t):
            @pl.when(me_x != t * stride)
            def _():
                copy_two(t).wait_send()

        loop(0, pieces, end_two)

        @pl.when(owner)
        def _():
            loop(1, nx, lambda s: copy_three(s, my_piece).wait_send())

        loop(1, ny, lambda s: copy_four(s).wait_send())


def on_device(
    nx,
    ny,
    block,
    features,
    edge_vec,
    edge_src,
    edge_dst,
    edge_count,
    send_gx,
    send_gy,
    w_one,
    w_two,
    mix,
    cotangent,
):
    owned, width = features.shape
    edges = edge_vec.shape[1]
    slots = send_gx.shape[1]
    hid = w_one.shape[1]
    rows = -(-(owned + 6 * slots) // CHUNK) * CHUNK
    chunks = rows // CHUNK
    vmem = pl.BlockSpec(memory_space=pltpu.VMEM)
    smem = pl.BlockSpec(memory_space=pltpu.SMEM)
    dma = pltpu.SemaphoreType.DMA
    pieces = SLICE // PIECE
    scratch = [
        pltpu.VMEM((rows, width), BF16),
        pltpu.VMEM((6 * slots, width), BF16),
        pltpu.VMEM((rows, width), BF16),
        pltpu.VMEM((6 * slots, width), BF16),
        pltpu.VMEM((CHUNK, chunks * width), F32),
        pltpu.VMEM((9 * width, owned), F32),
        pltpu.VMEM((9 * width, owned), BF16),
        pltpu.VMEM((CHUNK, edges), BF16),
        pltpu.VMEM((owned, edges), BF16),
        pltpu.VMEM((3 * width, edges), F32),
        pltpu.VMEM((3 * width, edges), F32),
        pltpu.VMEM((9 * width, edges), F32),
        pltpu.VMEM((hid, edges), F32),
        pltpu.VMEM((hid, edges), BF16),
        pltpu.VMEM((8, edges), F32),
        pltpu.VMEM((16, edges), BF16),
        pltpu.VMEM((8, edges), F32),
        pltpu.VMEM((8, edges), F32),
        pltpu.VMEM((1, edges), jnp.int32),
        pltpu.VMEM((8, edges), F32),
        pltpu.VMEM((1, edges), F32),
        pltpu.VMEM((hid, 3 * width), F32),
        pltpu.VMEM((16, hid), F32),
        pltpu.VMEM((8 * SLICE, width), F32),
        pltpu.VMEM((8 * SLICE, width), BF16),
        pltpu.VMEM((8, SLICE, width), BF16),
        pltpu.VMEM((SLICE, width), F32),
        pltpu.VMEM((32, PIECE, width), F32),
        pltpu.VMEM((PIECE, width), F32),
        pltpu.VMEM((SLICE, width), F32),
        pltpu.VMEM((SLICE, width), BF16),
        pltpu.VMEM((8 * SLICE, width), BF16),
        dma((6,)),
        dma((6,)),
        dma((6,)),
        dma((6,)),
        dma((8,)),
        dma((8,)),
        dma((pieces,)),
        dma((32,)),
        dma((32,)),
        dma((pieces,)),
        dma((8,)),
        dma((8,)),
    ]
    params = {"vmem_limit_bytes": 60 * 1024 * 1024}
    if nx > 1:
        params.update(collective_id=0, has_side_effects=True)
    return pl.pallas_call(
        functools.partial(kernel, nx, ny, block),
        out_shape=(
            jax.ShapeDtypeStruct((owned, 9 * width), BF16),
            jax.ShapeDtypeStruct((owned, width), F32),
            jax.ShapeDtypeStruct((3, edges), F32),
            jax.ShapeDtypeStruct(w_one.shape, F32),
            jax.ShapeDtypeStruct(w_two.shape, F32),
            jax.ShapeDtypeStruct(mix.shape, F32),
        ),
        in_specs=[vmem] * 4 + [smem] + [vmem] * 6,
        out_specs=(vmem,) * 6,
        scratch_shapes=scratch,
        compiler_params=pltpu.CompilerParams(**params),
        name="interaction",
    )(
        features,
        edge_vec,
        edge_src.reshape(1, edges),
        edge_dst.reshape(1, edges),
        edge_count,
        send_gx,
        send_gy,
        w_one,
        w_two,
        mix,
        cotangent,
    )


def solution(mesh, block=512):
    tiles = ("gx", "gy")
    return jax.shard_map(
        functools.partial(on_device, mesh.shape["gx"], mesh.shape["gy"], block),
        mesh=mesh,
        in_specs=(
            P(tiles, None),
            P(None, tiles),
            P(tiles),
            P(tiles),
            P(tiles),
            P(tiles, None),
            P(tiles, None),
            P(),
            P(),
            P(),
            P(tiles, None),
        ),
        out_specs=(
            P(tiles, None),
            P(tiles, None),
            P(None, tiles),
            P(),
            P(),
            P(),
        ),
        check_vma=False,
    )
```

```python
import functools
import math

import jax
import jax.numpy as jnp
from jax import lax
from jax.experimental import pallas as pl
from jax.experimental.pallas import tpu as pltpu
from jax.sharding import PartitionSpec as P

F32 = jnp.float32
BF16 = jnp.bfloat16
DEGREE = [0, 1, 1, 1, 2, 2, 2, 2, 2]
ROW_STEPS = [1, -1, 2, -2]
COLUMN_STEPS = [1, -1]
CHUNK = 256
SLICE = 32
SLICES = 19
PLANE_X = 4
SPREAD = 5
SPREAD_INVERSE = 13


def mm(a, b):
    return jnp.dot(a, b, preferred_element_type=F32)


def mm_nt(a, b):
    return lax.dot_general(a, b, (((1,), (1,)), ((), ())), preferred_element_type=F32)


def eye(n):
    rows = lax.broadcasted_iota(jnp.int32, (n, n), 0)
    cols = lax.broadcasted_iota(jnp.int32, (n, n), 1)
    return jnp.where(rows == cols, 1.0, 0.0).astype(BF16)


def split(a):
    hi = a.astype(BF16)
    lo = (a - hi.astype(F32)).astype(BF16)
    return hi, lo


def kernel(
    nx,
    ny,
    block,
    features,
    vec,
    src,
    dst,
    count,
    send_x,
    send_y,
    w_one,
    w_two,
    mix,
    cot_far,
    mixed_far,
    grad_feat,
    force,
    final,
    table,
    outgoing,
    dtab_out,
    back,
    dtab,
    acc,
    dacc,
    one_src,
    one_dst,
    radial,
    dweight,
    dterms,
    dsilu,
    hidden,
    harm,
    basis2,
    dbasis,
    geom,
    part,
    dharm,
    ddist,
    dw_two,
    dw_one,
    ar_half,
    got_one,
    got_two,
    half_three,
    cot,
    mixed,
    cot_sem,
    mixed_sem,
    ghost_send,
    ghost_recv,
    back_send,
    back_recv,
    one_send,
    one_recv,
    two_send,
    two_recv,
    three_send,
    three_recv,
    own_sem,
):
    owned, width = features.shape
    edges = vec.shape[1]
    slots = send_x.shape[1]
    comm = nx > 1
    chunks = table.shape[0] // CHUNK
    me_x = lax.axis_index("gx")
    me_y = lax.axis_index("gy")
    factor = math.sqrt(owned / edges)
    group = PLANE_X * ny
    planes = nx // PLANE_X
    plane = lax.div(me_x, PLANE_X)
    member = lax.rem(me_x, PLANE_X) * ny + me_y
    my_slice = lax.rem(member * SPREAD_INVERSE, group)
    owner = my_slice < SLICES

    def loop(low, high, f):
        def step(s, c):
            f(s)
            return c

        lax.fori_loop(low, high, step, 0)

    def in_plane(u):
        return {"gx": plane * PLANE_X + lax.div(u, ny), "gy": lax.rem(u, ny)}

    def along(s):
        return {"gx": lax.rem(me_x + s + nx, nx)}

    def across(s):
        return {"gy": lax.rem(me_y + s + ny, ny)}

    if comm:
        barrier = pltpu.get_barrier_semaphore()

        def greet(where):
            pl.semaphore_signal(barrier, inc=1, device_id=where, device_id_type=pl.DeviceIdType.MESH)

        loop(1, group, lambda s: greet(in_plane(lax.rem(member + s, group))))
        loop(1, planes, lambda s: greet(along(s * PLANE_X)))
        for s in ROW_STEPS:
            greet(along(s))

    cot_copy = pltpu.make_async_copy(cot_far, cot, cot_sem)
    cot_copy.start()

    def remote(where, source, target, send, recv):
        return pltpu.make_async_remote_copy(
            src_ref=source,
            dst_ref=target,
            send_sem=send,
            recv_sem=recv,
            device_id=where,
            device_id_type=pl.DeviceIdType.MESH,
        )

    def to_peer(p, source, target, sends, recvs, sign):
        where = along(sign * ROW_STEPS[p]) if p < 4 else across(sign * COLUMN_STEPS[p - 4])
        if not comm:
            return pltpu.make_async_copy(source, target, recvs.at[p])
        return remote(where, source, target, sends.at[p], recvs.at[p])

    eye256 = eye(256)
    eye128 = eye256[:128, :128]
    feats = features[...]

    def picks(p):
        row = send_x[p : p + 1, :] if p < 4 else send_y[p - 4 : p - 3, :]
        rows = lax.broadcasted_iota(jnp.int32, (owned, slots), 0)
        return jnp.where(rows == row, 1.0, 0.0).astype(BF16)

    eye_slots = eye256[:slots, :slots]
    for p in range(6):
        pick = mm_nt(eye_slots, picks(p)).astype(BF16)
        outgoing[p * slots : (p + 1) * slots, :] = mm(pick, feats).astype(BF16)
    if comm:
        pl.semaphore_wait(barrier, group + planes + len(ROW_STEPS) - 2)
    ghosts = [
        to_peer(
            p,
            outgoing.at[pl.ds(p * slots, slots)],
            table.at[pl.ds(owned + p * slots, slots)],
            ghost_send,
            ghost_recv,
            1,
        )
        for p in range(6)
    ]
    for copy in ghosts:
        copy.start()

    table[0:owned, :] = feats
    used = owned + 6 * slots
    table[used:, :] = jnp.zeros((table.shape[0] - used, width), BF16)
    dtab[...] = jnp.zeros_like(dtab)
    acc[...] = jnp.zeros_like(acc)
    dw_two[...] = jnp.zeros_like(dw_two)
    dw_one[...] = jnp.zeros_like(dw_one)

    w1h, w1l = split(w_one[...])
    w1h = w1h.astype(F32)
    w1l = w1l.astype(F32)
    w1_both = jnp.concatenate([w1h, w1l], axis=0).astype(BF16)
    w1_stack = jnp.concatenate([w1h, w1h, w1l, jnp.zeros_like(w1l)], axis=0).astype(BF16)
    w1_t = mm_nt(eye256[:64, :64], w1_stack).astype(BF16)
    w2h, w2l = split(w_two[...])
    w2_both = jnp.concatenate([w2h, w2l], axis=0)
    w2_stack = jnp.concatenate([w2h, w2h, w2l], axis=0)
    w2_t = jnp.concatenate(
        [mm_nt(eye128, w2_stack[:, deg * width : (deg + 1) * width]).astype(BF16) for deg in range(3)],
        axis=0,
    )
    mix_hl = [split(mix[deg]) for deg in range(3)]
    cot_copy.wait()
    for m in range(9):
        hi, lo = mix_hl[DEGREE[m]]
        cot_m = cot[:, m * width : (m + 1) * width]
        both = mm_nt(jnp.concatenate([hi, lo], axis=1), jnp.concatenate([cot_m, cot_m], axis=1))
        dacc[m * width : (m + 1) * width, :] = (both * factor).astype(BF16)

    live_count = count[0]
    r3 = math.sqrt(3.0)
    r5 = math.sqrt(5.0)
    r15 = math.sqrt(15.0)
    pi = math.pi

    def part_one(b, carry):
        start = pl.multiple_of(b * block, block)
        sl = pl.ds(start, block)
        index = src[:, sl]
        chunk = lax.shift_right_logical(index, 8)
        part[:, sl] = chunk
        rows = lax.broadcasted_iota(jnp.int32, (CHUNK, block), 0)
        one_src[:, sl] = jnp.where(rows == index - chunk * CHUNK, 1.0, 0.0).astype(BF16)
        one_dst[:, sl] = jnp.where(rows == dst[:, sl], 1.0, 0.0).astype(BF16)
        dall = mm(dacc[...], one_dst[:, sl])
        dterms[:, sl] = dall.astype(BF16)

        v = vec[:, sl]
        x, y, z = v[0:1], v[1:2], v[2:3]
        dist = jnp.sqrt(x * x + y * y + z * z + 0.25)
        inv = 1.0 / dist
        ratio = dist * (1.0 / 5.0)
        ra2 = ratio * ratio
        ra5 = ra2 * ra2 * ratio
        env = 1.0 / (1.0 + ra5 * ratio)
        ux, uy, uz = x * inv, y * inv, z * inv
        geom[0:1, sl] = ux
        geom[1:2, sl] = uy
        geom[2:3, sl] = uz
        geom[3:4, sl] = inv
        hs = [
            r3 * ux,
            r3 * uy,
            r3 * uz,
            r15 * ux * uy,
            r15 * uy * uz,
            0.5 * r5 * (3.0 * uz * uz - 1.0),
            r15 * ux * uz,
            0.5 * r15 * (ux * ux - uy * uy),
        ]
        for i in range(8):
            harm[i : i + 1, sl] = hs[i]
        k = (lax.broadcasted_iota(jnp.int32, (8, block), 0) + 1).astype(F32)
        t = k * ratio
        n = jnp.floor(t + 0.5)
        r = t - n
        sgn = 1.0 - 2.0 * (n - 2.0 * jnp.floor(n * 0.5))
        q = r * r
        s_pi = pi**9 / 362880.0 - q * (pi**11 / 39916800.0)
        s_pi = pi**7 / 5040.0 - q * s_pi
        s_pi = pi**5 / 120.0 - q * s_pi
        s_pi = pi**3 / 6.0 - q * s_pi
        s_pi = r * (pi - q * s_pi)
        c_pi = pi**10 / 3628800.0 - q * (pi**12 / 479001600.0)
        c_pi = pi**8 / 40320.0 - q * c_pi
        c_pi = pi**6 / 720.0 - q * c_pi
        c_pi = pi**4 / 24.0 - q * c_pi
        c_pi = pi**2 / 2.0 - q * c_pi
        c_pi = 1.0 - q * c_pi
        amp = sgn * (inv * env)
        bas = s_pi * amp
        dbasis[:, sl] = c_pi * amp * (k * (pi / 5.0)) - bas * (inv + (6.0 / 5.0) * (env * ra5))
        bh = bas.astype(BF16).astype(F32)
        bl = bas - bh
        basis2[:, sl] = jnp.concatenate([bh, bl], axis=0).astype(BF16)
        bstack = jnp.concatenate([bh, bl, bh, jnp.zeros_like(bh)], axis=0).astype(BF16)
        pre = mm(w1_t, bstack)
        spot = lax.broadcasted_iota(jnp.int32, (1, block), 1) + start
        live = jnp.where(spot < live_count, 1.0, 0.0)
        sig = 1.0 / (1.0 + jnp.exp(-pre))
        sig_live = sig * live
        hid = pre * sig_live
        dsilu[:, sl] = sig_live * (1.0 + pre * (1.0 - sig))
        hh, hl = split(hid)
        hidden[:, sl] = hh
        rad = mm(w2_t, jnp.concatenate([hh, hl, hh], axis=0))
        radial[:, sl] = rad

        dg = None
        for deg, ms in enumerate(((0,), (1, 2, 3), (4, 5, 6, 7, 8))):
            total = None
            for m in ms:
                term = dall[m * width : (m + 1) * width]
                if m > 0:
                    term = term * hs[m - 1]
                total = term if total is None else total + term
            dweight[deg * width : (deg + 1) * width, sl] = total
            one = rad[deg * width : (deg + 1) * width] * total
            dg = one if dg is None else dg + one
        dgm = jnp.concatenate([jnp.where(chunk == c, dg, 0.0).astype(BF16) for c in range(chunks)], axis=0)
        dtab[...] += mm_nt(one_src[:, sl], dgm)
        return carry

    lax.fori_loop(0, edges // block, part_one, 0)

    for c in range(chunks):
        dtab_out[c * CHUNK : (c + 1) * CHUNK, :] = dtab[:, c * width : (c + 1) * width].astype(BF16)
    returns = [
        to_peer(
            p,
            dtab_out.at[pl.ds(owned + p * slots, slots)],
            back.at[pl.ds(p * slots, slots)],
            back_send,
            back_recv,
            -1,
        )
        for p in range(6)
    ]
    for copy in returns:
        copy.start()

    for copy in ghosts:
        if comm:
            copy.wait_recv()
        else:
            copy.wait()
    table_t = jnp.concatenate(
        [mm_nt(eye128, table[c * CHUNK : (c + 1) * CHUNK, :]).astype(BF16) for c in range(chunks)], axis=0
    )

    def part_two(b, carry):
        start = pl.multiple_of(b * block, block)
        sl = pl.ds(start, block)
        chunk = part[:, sl]
        got = mm(table_t, one_src[:, sl])
        g = got[0:width]
        for c in range(1, chunks):
            g = jnp.where(chunk == c, got[c * width : (c + 1) * width], g)
        drad = jnp.concatenate(
            [(dweight[deg * width : (deg + 1) * width, sl] * g).astype(BF16) for deg in range(3)], axis=0
        )
        weighted = [radial[deg * width : (deg + 1) * width, sl] * g for deg in range(3)]
        for deg in range(3):
            radial[deg * width : (deg + 1) * width, sl] = weighted[deg]
        terms = [weighted[0].astype(BF16)]
        for m in range(1, 9):
            terms.append((weighted[DEGREE[m]] * harm[m - 1 : m, sl]).astype(BF16))
        dhid = mm(w2_both, drad)
        dw_two[...] += mm_nt(hidden[:, sl], drad)
        acc[...] += mm_nt(jnp.concatenate(terms, axis=0), one_dst[:, sl])
        dpre = ((dhid[:64] + dhid[64:]) * dsilu[:, sl]).astype(BF16)
        dw_one[...] += mm_nt(basis2[:, sl], dpre)
        dbas = mm(w1_both, dpre)
        ddist[:, sl] = jnp.sum((dbas[:8] + dbas[8:]) * dbasis[:, sl], axis=0, keepdims=True)
        return carry

    lax.fori_loop(0, edges // block, part_two, 0)

    accb = [(acc[m * width : (m + 1) * width, :] * factor).astype(BF16) for m in range(9)]
    for deg in range(3):
        total = None
        for m in range(9):
            if DEGREE[m] == deg:
                one = mm(accb[m], cot[:, m * width : (m + 1) * width])
                total = one if total is None else total + one
        ar_half[deg * width : (deg + 1) * width, :] = total.astype(BF16)
    row = 3 * width
    for deg in range(3):
        ar_half[row : row + 64, :] = dw_two[:, deg * width : (deg + 1) * width].astype(BF16)
        row += 64
    tail = jnp.concatenate([dw_one[0:8, :] + dw_one[8:16, :], jnp.zeros((8, 64), F32)], axis=0)
    tail = jnp.concatenate([tail, jnp.zeros((16, 64), F32)], axis=1)
    ar_half[row : row + 16, :] = tail.astype(BF16)
    ar_half[row + 16 :, :] = jnp.zeros((ar_half.shape[0] - row - 16, width), BF16)

    def rows_of(q):
        return pl.ds(pl.multiple_of(q * SLICE, SLICE), SLICE)

    def copy_one(q):
        u = lax.rem(q * SPREAD, group)
        slot = lax.rem(member - u + group, group)
        return remote(in_plane(u), ar_half.at[rows_of(q)], got_one.at[slot], one_send, one_recv)

    def copy_two(s):
        return remote(along(s * PLANE_X), got_two.at[plane], got_two.at[plane], two_send, two_recv)

    def copy_three(s):
        where = in_plane(lax.rem(member + s, group))
        return remote(where, half_three, final.at[rows_of(my_slice)], three_send, three_recv)

    here = {"gx": me_x, "gy": me_y}
    all_one = remote(here, got_one.at[pl.ds(1, group - 1)], got_one.at[pl.ds(1, group - 1)], one_send, one_recv)
    all_two = remote(here, got_two.at[pl.ds(1, planes - 1)], got_two.at[pl.ds(1, planes - 1)], two_send, two_recv)
    most = pl.ds(0, (SLICES - 1) * SLICE)
    all_rows = remote(here, ar_half, final, one_send, three_recv)
    most_rows = remote(here, ar_half.at[most], final.at[most], one_send, three_recv)

    if comm:

        def send_one(q):
            @pl.when(q != my_slice)
            def _():
                copy_one(q).start()

        loop(0, SLICES, send_one)

    def sums(b, carry):
        sl = pl.ds(pl.multiple_of(b * 256, 256), 256)
        for deg in range(3):
            w = radial[deg * width : (deg + 1) * width, sl]
            for m in range(1, 9):
                if DEGREE[m] == deg:
                    d = dterms[m * width : (m + 1) * width, sl].astype(F32)
                    dharm[m - 1 : m, sl] = jnp.sum(w * d, axis=0, keepdims=True)
        return carry

    lax.fori_loop(0, edges // 256, sums, 0)

    if comm:

        @pl.when(owner)
        def _():
            all_one.wait_recv()
            total = ar_half[rows_of(my_slice), :].astype(F32)
            for s in range(1, group):
                total = total + got_one[s].astype(F32)
            got_two[plane] = total
            loop(1, planes, lambda s: copy_two(s).start())

    ux, uy, uz, inv = (geom[i : i + 1, :] for i in range(4))
    g1, g2, g3, g4, g5, g6, g7, g8 = (dharm[i : i + 1, :] for i in range(8))
    dx = r3 * g1 + r15 * (g4 * uy + g7 * uz + g8 * ux)
    dy = r3 * g2 + r15 * (g4 * ux + g5 * uz - g8 * uy)
    dz = r3 * g3 + r15 * (g5 * uy + g7 * ux) + (3.0 * r5) * (uz * g6)
    dd = ddist[...] - (dx * ux + dy * uy + dz * uz) * inv
    force[0:1, :] = dx * inv + ux * dd
    force[1:2, :] = dy * inv + uy * dd
    force[2:3, :] = dz * inv + uz * dd

    for deg in range(3):
        hi, lo = mix_hl[deg]
        mix_t = jnp.concatenate([mm_nt(eye128, hi), mm_nt(eye128, lo)], axis=1).astype(BF16)
        for m in range(9):
            if DEGREE[m] == deg:
                out_t = mm(mix_t, jnp.concatenate([accb[m], accb[m]], axis=0)).astype(BF16)
                mixed[:, m * width : (m + 1) * width] = mm_nt(eye256, out_t).astype(BF16)
    mixed_copy = pltpu.make_async_copy(mixed, mixed_far, mixed_sem)
    mixed_copy.start()

    if comm:

        @pl.when(owner)
        def _():
            all_two.wait_recv()
            total = got_two[0]
            for s in range(1, planes):
                total = total + got_two[s]
            half_three[...] = total.astype(BF16)
            loop(1, group, lambda s: copy_three(s).start())
            own = pltpu.make_async_copy(half_three, final.at[rows_of(my_slice)], own_sem)
            own.start()
            own.wait()

    for copy in returns:
        if comm:
            copy.wait_recv()
        else:
            copy.wait()
    total = dtab[:, 0:width]
    for p in range(6):
        total = total + mm(picks(p), back[p * slots : (p + 1) * slots, :])
    grad_feat[...] = total

    if comm:
        for copy in ghosts:
            copy.wait_send()
        for copy in returns:
            copy.wait_send()

        @pl.when(owner)
        def _():
            most_rows.wait_send()
            all_two.wait_send()
            loop(1, group, lambda s: copy_three(s).wait_send())
            most_rows.wait_recv()

        @pl.when(jnp.logical_not(owner))
        def _():
            all_rows.wait_send()
            all_rows.wait_recv()

    else:
        own = pltpu.make_async_copy(ar_half, final, own_sem)
        own.start()
        own.wait()
    mixed_copy.wait()


def finish(mixed_in, feat_in, force_in, rows, mixed, grad_feat, force, grad_one, grad_two, grad_mix, sems):
    width = rows.shape[1]
    copies = [
        pltpu.make_async_copy(a, b, sems.at[i])
        for i, (a, b) in enumerate(((mixed_in, mixed), (feat_in, grad_feat), (force_in, force)))
    ]
    for copy in copies:
        copy.start()
    for deg in range(3):
        grad_mix[deg] = rows[deg * width : (deg + 1) * width, :].astype(F32)
    row = 3 * width
    for deg in range(3):
        grad_two[:, deg * width : (deg + 1) * width] = rows[row : row + 64, :].astype(F32)
        row += 64
    grad_one[...] = rows[row : row + 16, :].astype(F32)[0:8, 0:64]
    for copy in copies:
        copy.wait()


def on_device(
    nx,
    ny,
    block,
    features,
    edge_vec,
    edge_src,
    edge_dst,
    edge_count,
    send_gx,
    send_gy,
    w_one,
    w_two,
    mix,
    cotangent,
):
    owned, width = features.shape
    edges = edge_vec.shape[1]
    slots = send_gx.shape[1]
    hid = w_one.shape[1]
    rows = -(-(owned + 6 * slots) // CHUNK) * CHUNK
    chunks = rows // CHUNK
    group = PLANE_X * ny
    planes = max(nx // PLANE_X, 2)
    vmem = pl.BlockSpec(memory_space=pltpu.VMEM)
    smem = pl.BlockSpec(memory_space=pltpu.SMEM)
    far = pl.BlockSpec(memory_space=pl.ANY)
    dma = pltpu.SemaphoreType.DMA
    scratch = [
        pltpu.VMEM((rows, width), BF16),
        pltpu.VMEM((6 * slots, width), BF16),
        pltpu.VMEM((rows, width), BF16),
        pltpu.VMEM((6 * slots, width), BF16),
        pltpu.VMEM((CHUNK, chunks * width), F32),
        pltpu.VMEM((9 * width, owned), F32),
        pltpu.VMEM((9 * width, owned), BF16),
        pltpu.VMEM((CHUNK, edges), BF16),
        pltpu.VMEM((owned, edges), BF16),
        pltpu.VMEM((3 * width, edges), F32),
        pltpu.VMEM((3 * width, edges), F32),
        pltpu.VMEM((9 * width, edges), BF16),
        pltpu.VMEM((hid, edges), F32),
        pltpu.VMEM((hid, edges), BF16),
        pltpu.VMEM((8, edges), F32),
        pltpu.VMEM((16, edges), BF16),
        pltpu.VMEM((8, edges), F32),
        pltpu.VMEM((8, edges), F32),
        pltpu.VMEM((1, edges), jnp.int32),
        pltpu.VMEM((8, edges), F32),
        pltpu.VMEM((1, edges), F32),
        pltpu.VMEM((hid, 3 * width), F32),
        pltpu.VMEM((16, hid), F32),
        pltpu.VMEM((SLICES * SLICE, width), BF16),
        pltpu.VMEM((group, SLICE, width), BF16),
        pltpu.VMEM((planes, SLICE, width), F32),
        pltpu.VMEM((SLICE, width), BF16),
        pltpu.VMEM((owned, 9 * width), BF16),
        pltpu.VMEM((owned, 9 * width), BF16),
        dma,
        dma,
        dma((6,)),
        dma((6,)),
        dma((6,)),
        dma((6,)),
        dma,
        dma,
        dma,
        dma,
        dma,
        dma,
        dma,
    ]
    params = {"vmem_limit_bytes": 60 * 1024 * 1024}
    if nx > 1:
        params.update(collective_id=0, has_side_effects=True)
    shapes = (
        jax.ShapeDtypeStruct((owned, 9 * width), BF16),
        jax.ShapeDtypeStruct((owned, width), F32),
        jax.ShapeDtypeStruct((3, edges), F32),
    )
    mixed, grad_feat, force, final = pl.pallas_call(
        functools.partial(kernel, nx, ny, block),
        out_shape=(*shapes, jax.ShapeDtypeStruct((SLICES * SLICE, width), BF16)),
        in_specs=[vmem] * 4 + [smem] + [vmem] * 5 + [far],
        out_specs=(far, vmem, vmem, far),
        scratch_shapes=scratch,
        compiler_params=pltpu.CompilerParams(**params),
        name="interaction",
    )(
        features,
        edge_vec,
        edge_src.reshape(1, edges),
        edge_dst.reshape(1, edges),
        edge_count,
        send_gx,
        send_gy,
        w_one,
        w_two,
        mix,
        cotangent,
    )
    return pl.pallas_call(
        finish,
        out_shape=(
            *shapes,
            jax.ShapeDtypeStruct(w_one.shape, F32),
            jax.ShapeDtypeStruct(w_two.shape, F32),
            jax.ShapeDtypeStruct(mix.shape, F32),
        ),
        in_specs=[vmem] * 4,
        out_specs=(far, far, far, vmem, vmem, vmem),
        scratch_shapes=[dma((3,))],
        name="finish",
    )(mixed, grad_feat, force, final)


def solution(mesh, block=1024):
    tiles = ("gx", "gy")
    return jax.shard_map(
        functools.partial(on_device, mesh.shape["gx"], mesh.shape["gy"], block),
        mesh=mesh,
        in_specs=(
            P(tiles, None),
            P(None, tiles),
            P(tiles),
            P(tiles),
            P(tiles),
            P(tiles, None),
            P(tiles, None),
            P(),
            P(),
            P(),
            P(tiles, None),
        ),
        out_specs=(
            P(tiles, None),
            P(tiles, None),
            P(None, tiles),
            P(),
            P(),
            P(),
        ),
        check_vma=False,
    )
```

```python
import functools
import math

import jax
import jax.numpy as jnp
from jax import lax
from jax.experimental import pallas as pl
from jax.experimental.pallas import tpu as pltpu
from jax.sharding import PartitionSpec as P

F32 = jnp.float32
BF16 = jnp.bfloat16
DEGREE = [0, 1, 1, 1, 2, 2, 2, 2, 2]
ROW_STEPS = [1, -1, 2, -2]
COLUMN_STEPS = [1, -1]
CHUNK = 256
SLICE = 32
SLICES = 19
PLANE_X = 4
SPREAD = 5
SPREAD_INVERSE = 13


def mm(a, b):
    return jnp.dot(a, b, preferred_element_type=F32)


def mm_nt(a, b):
    return lax.dot_general(a, b, (((1,), (1,)), ((), ())), preferred_element_type=F32)


def eye(n):
    rows = lax.broadcasted_iota(jnp.int32, (n, n), 0)
    cols = lax.broadcasted_iota(jnp.int32, (n, n), 1)
    return jnp.where(rows == cols, 1.0, 0.0).astype(BF16)


def split(a):
    hi = a.astype(BF16)
    lo = (a - hi.astype(F32)).astype(BF16)
    return hi, lo


def kernel(
    nx,
    ny,
    block,
    *refs,
):
    inputs = refs[:11]
    mixed_far, grad_feat_far, force_far, final = refs[11:15]
    near = refs[15:26]
    (
        features,
        vec,
        src,
        dst,
        count,
        send_x,
        send_y,
        w_one,
        w_two,
        mix,
        cot,
    ) = near
    (
        mixed,
        grad_feat,
        force,
        table,
        outgoing,
        dtab_out,
        back,
        dtab,
        acc,
        dacc,
        one_src,
        one_dst,
        radial,
        dweight,
        dterms,
        dsilu,
        hidden,
        harm,
        basis2,
        dbasis,
        geom,
        part,
        dharm,
        dw_two,
        dpre,
        gathered,
        ar_half,
        got_one,
        got_two,
        half_three,
        ghost_send,
        ghost_recv,
        back_send,
        back_recv,
        one_send,
        one_recv,
        two_send,
        two_recv,
        three_send,
        three_recv,
        own_sem,
        in_sem,
        out_sem,
    ) = refs[26:]
    owned, width = features.shape
    edges = vec.shape[1]
    slots = send_x.shape[1]
    comm = nx > 1
    chunks = table.shape[0] // CHUNK
    me_x = lax.axis_index("gx")
    me_y = lax.axis_index("gy")
    factor = math.sqrt(owned / edges)
    group = PLANE_X * ny
    planes = nx // PLANE_X
    plane = lax.div(me_x, PLANE_X)
    member = lax.rem(me_x, PLANE_X) * ny + me_y
    my_slice = lax.rem(member * SPREAD_INVERSE, group)
    owner = my_slice < SLICES

    def loop(low, high, f):
        def step(s, c):
            f(s)
            return c

        lax.fori_loop(low, high, step, 0)

    def in_plane(u):
        return {"gx": plane * PLANE_X + lax.div(u, ny), "gy": lax.rem(u, ny)}

    def along(s):
        return {"gx": lax.rem(me_x + s + nx, nx)}

    def across(s):
        return {"gy": lax.rem(me_y + s + ny, ny)}

    if comm:
        barrier = pltpu.get_barrier_semaphore()

        def greet(where):
            pl.semaphore_signal(barrier, inc=1, device_id=where, device_id_type=pl.DeviceIdType.MESH)

        loop(1, group, lambda s: greet(in_plane(lax.rem(member + s, group))))
        loop(1, planes, lambda s: greet(along(s * PLANE_X)))
        for s in ROW_STEPS:
            greet(along(s))

    loads = [pltpu.make_async_copy(a, b, in_sem.at[i]) for i, (a, b) in enumerate(zip(inputs, near))]
    for i in (0, 5, 6, 10, 9, 8, 7, 1, 2, 3, 4):
        loads[i].start()

    def remote(where, source, target, send, recv):
        return pltpu.make_async_remote_copy(
            src_ref=source,
            dst_ref=target,
            send_sem=send,
            recv_sem=recv,
            device_id=where,
            device_id_type=pl.DeviceIdType.MESH,
        )

    def to_peer(p, source, target, sends, recvs, sign):
        where = along(sign * ROW_STEPS[p]) if p < 4 else across(sign * COLUMN_STEPS[p - 4])
        if not comm:
            return pltpu.make_async_copy(source, target, recvs.at[p])
        return remote(where, source, target, sends.at[p], recvs.at[p])

    eye256 = eye(256)
    eye128 = eye256[:128, :128]
    for i in (0, 5, 6):
        loads[i].wait()
    feats = features[...]

    def picks(p):
        row = send_x[p : p + 1, :] if p < 4 else send_y[p - 4 : p - 3, :]
        rows = lax.broadcasted_iota(jnp.int32, (owned, slots), 0)
        return jnp.where(rows == row, 1.0, 0.0).astype(BF16)

    eye_slots = eye256[:slots, :slots]
    for p in range(6):
        pick = mm_nt(eye_slots, picks(p)).astype(BF16)
        outgoing[p * slots : (p + 1) * slots, :] = mm(pick, feats).astype(BF16)
    if comm:
        pl.semaphore_wait(barrier, group + planes + len(ROW_STEPS) - 2)
    ghosts = [
        to_peer(
            p,
            outgoing.at[pl.ds(p * slots, slots)],
            table.at[pl.ds(owned + p * slots, slots)],
            ghost_send,
            ghost_recv,
            1,
        )
        for p in range(6)
    ]
    for copy in ghosts:
        copy.start()

    dtab[...] = jnp.zeros_like(dtab)
    acc[...] = jnp.zeros_like(acc)
    dw_two[...] = jnp.zeros_like(dw_two)
    table[0:owned, :] = feats
    used = owned + 6 * slots
    table[used:, :] = jnp.zeros((table.shape[0] - used, width), BF16)

    for i in (7, 8, 9, 1, 2, 3, 4):
        loads[i].wait()
    w1h, w1l = split(w_one[...])
    w1h = w1h.astype(F32)
    w1l = w1l.astype(F32)
    w1_both = jnp.concatenate([w1h, w1l], axis=0).astype(BF16)
    w1_stack = jnp.concatenate([w1h, w1h, w1l, jnp.zeros_like(w1l)], axis=0).astype(BF16)
    w1_t = mm_nt(eye256[:64, :64], w1_stack).astype(BF16)
    w2h, w2l = split(w_two[...])
    w2_both = jnp.concatenate([w2h, w2l], axis=0)
    w2_stack = jnp.concatenate([w2h, w2h, w2l], axis=0)
    w2_t = jnp.concatenate(
        [mm_nt(eye128, w2_stack[:, deg * width : (deg + 1) * width]).astype(BF16) for deg in range(3)],
        axis=0,
    )
    mix_hl = [split(mix[deg]) for deg in range(3)]
    loads[10].wait()
    for m in range(9):
        hi, lo = mix_hl[DEGREE[m]]
        cot_m = cot[:, m * width : (m + 1) * width]
        both = mm_nt(jnp.concatenate([hi, lo], axis=1), jnp.concatenate([cot_m, cot_m], axis=1))
        dacc[m * width : (m + 1) * width, :] = (both * factor).astype(BF16)

    live_count = count[...]
    r3 = math.sqrt(3.0)
    r5 = math.sqrt(5.0)
    r15 = math.sqrt(15.0)
    pi = math.pi

    def part_one(b, carry):
        start = pl.multiple_of(b * block, block)
        sl = pl.ds(start, block)
        index = src[:, sl]
        chunk = lax.shift_right_logical(index, 8)
        part[:, sl] = chunk
        rows = lax.broadcasted_iota(jnp.int32, (CHUNK, block), 0)
        one_src[:, sl] = jnp.where(rows == index - chunk * CHUNK, 1.0, 0.0).astype(BF16)
        one_dst[:, sl] = jnp.where(rows == dst[:, sl], 1.0, 0.0).astype(BF16)
        dall = mm(dacc[...], one_dst[:, sl])
        dterms[:, sl] = dall.astype(BF16)

        v = vec[:, sl]
        x, y, z = v[0:1], v[1:2], v[2:3]
        dist = jnp.sqrt(x * x + y * y + z * z + 0.25)
        inv = 1.0 / dist
        ratio = dist * (1.0 / 5.0)
        ra2 = ratio * ratio
        ra5 = ra2 * ra2 * ratio
        env = 1.0 / (1.0 + ra5 * ratio)
        ux, uy, uz = x * inv, y * inv, z * inv
        geom[0:1, sl] = ux
        geom[1:2, sl] = uy
        geom[2:3, sl] = uz
        geom[3:4, sl] = inv
        hs = [
            r3 * ux,
            r3 * uy,
            r3 * uz,
            r15 * ux * uy,
            r15 * uy * uz,
            0.5 * r5 * (3.0 * uz * uz - 1.0),
            r15 * ux * uz,
            0.5 * r15 * (ux * ux - uy * uy),
        ]
        for i in range(8):
            harm[i : i + 1, sl] = hs[i]
        k = (lax.broadcasted_iota(jnp.int32, (8, block), 0) + 1).astype(F32)
        t = k * ratio
        n = jnp.floor(t + 0.5)
        r = t - n
        sgn = 1.0 - 2.0 * (n - 2.0 * jnp.floor(n * 0.5))
        q = r * r
        s_pi = pi**9 / 362880.0 - q * (pi**11 / 39916800.0)
        s_pi = pi**7 / 5040.0 - q * s_pi
        s_pi = pi**5 / 120.0 - q * s_pi
        s_pi = pi**3 / 6.0 - q * s_pi
        s_pi = r * (pi - q * s_pi)
        c_pi = pi**10 / 3628800.0 - q * (pi**12 / 479001600.0)
        c_pi = pi**8 / 40320.0 - q * c_pi
        c_pi = pi**6 / 720.0 - q * c_pi
        c_pi = pi**4 / 24.0 - q * c_pi
        c_pi = pi**2 / 2.0 - q * c_pi
        c_pi = 1.0 - q * c_pi
        amp = sgn * (inv * env)
        bas = s_pi * amp
        dbasis[:, sl] = c_pi * amp * (k * (pi / 5.0)) - bas * (inv + (6.0 / 5.0) * (env * ra5))
        bh = bas.astype(BF16).astype(F32)
        bl = bas - bh
        basis2[:, sl] = jnp.concatenate([bh, bl], axis=0).astype(BF16)
        bstack = jnp.concatenate([bh, bl, bh, jnp.zeros_like(bh)], axis=0).astype(BF16)
        pre = mm(w1_t, bstack)
        spot = lax.broadcasted_iota(jnp.int32, (1, block), 1) + start
        live = jnp.where(spot < live_count, 1.0, 0.0)
        sig = 1.0 / (1.0 + jnp.exp(-pre))
        sig_live = sig * live
        hid = pre * sig_live
        dsilu[:, sl] = sig_live * (1.0 + pre * (1.0 - sig))
        hh, hl = split(hid)
        hidden[:, sl] = hh
        radial[:, sl] = mm(w2_t, jnp.concatenate([hh, hl, hh], axis=0))

        for deg, ms in enumerate(((0,), (1, 2, 3), (4, 5, 6, 7, 8))):
            total = None
            for m in ms:
                term = dall[m * width : (m + 1) * width]
                if m > 0:
                    term = term * hs[m - 1]
                total = term if total is None else total + term
            dweight[deg * width : (deg + 1) * width, sl] = total
        return carry

    lax.fori_loop(0, edges // block, part_one, 0)

    for copy in ghosts:
        if comm:
            copy.wait_recv()
        else:
            copy.wait()
    table_t = jnp.concatenate(
        [mm_nt(eye128, table[c * CHUNK : (c + 1) * CHUNK, :]).astype(BF16) for c in range(chunks)], axis=0
    )

    def gather(b):
        sl = pl.ds(pl.multiple_of(b * block, block), block)
        chunk = part[:, sl]
        got = mm(table_t, one_src[:, sl])
        g = got[0:width]
        for c in range(1, chunks):
            g = jnp.where(chunk == c, got[c * width : (c + 1) * width], g)
        gathered[:, sl] = g

    def part_two(b, carry):
        sl = pl.ds(pl.multiple_of(b * block, block), block)
        gather(b)
        g = gathered[:, sl]
        drad = jnp.concatenate(
            [(dweight[deg * width : (deg + 1) * width, sl] * g).astype(BF16) for deg in range(3)], axis=0
        )
        weighted = [radial[deg * width : (deg + 1) * width, sl] * g for deg in range(3)]
        terms = [weighted[0].astype(BF16)]
        for m in range(1, 9):
            terms.append((weighted[DEGREE[m]] * harm[m - 1 : m, sl]).astype(BF16))
        dhid = mm(w2_both, drad)
        dw_two[...] += mm_nt(hidden[:, sl], drad)
        acc[...] += (mm_nt(jnp.concatenate(terms, axis=0), one_dst[:, sl]))
        dpre[:, sl] = ((dhid[:64] + dhid[64:]) * dsilu[:, sl]).astype(BF16)
        return carry

    lax.fori_loop(0, edges // block, part_two, 0)
    dw_one = mm_nt(basis2[...], dpre[...])

    accb = [(acc[m * width : (m + 1) * width, :] * factor).astype(BF16) for m in range(9)]
    for deg in range(3):
        total = None
        for m in range(9):
            if DEGREE[m] == deg:
                one = mm(accb[m], cot[:, m * width : (m + 1) * width])
                total = one if total is None else total + one
        ar_half[deg * width : (deg + 1) * width, :] = total.astype(BF16)
    row = 3 * width
    for deg in range(3):
        ar_half[row : row + 64, :] = dw_two[:, deg * width : (deg + 1) * width].astype(BF16)
        row += 64
    tail = jnp.concatenate([dw_one[0:8, :] + dw_one[8:16, :], jnp.zeros((8, 64), F32)], axis=0)
    tail = jnp.concatenate([tail, jnp.zeros((16, 64), F32)], axis=1)
    ar_half[row : row + 16, :] = tail.astype(BF16)
    ar_half[row + 16 :, :] = jnp.zeros((ar_half.shape[0] - row - 16, width), BF16)

    def rows_of(q):
        return pl.ds(pl.multiple_of(q * SLICE, SLICE), SLICE)

    def copy_one(q):
        u = lax.rem(q * SPREAD, group)
        slot = lax.rem(member - u + group, group)
        return remote(in_plane(u), ar_half.at[rows_of(q)], got_one.at[slot], one_send, one_recv)

    def copy_two(s):
        return remote(along(s * PLANE_X), got_two.at[plane], got_two.at[plane], two_send, two_recv)

    def copy_three(s):
        where = in_plane(lax.rem(member + s, group))
        return remote(where, half_three, final.at[rows_of(my_slice)], three_send, three_recv)

    here = {"gx": me_x, "gy": me_y}
    all_one = remote(here, got_one.at[pl.ds(1, group - 1)], got_one.at[pl.ds(1, group - 1)], one_send, one_recv)
    all_two = remote(here, got_two.at[pl.ds(1, planes - 1)], got_two.at[pl.ds(1, planes - 1)], two_send, two_recv)
    most = pl.ds(0, (SLICES - 1) * SLICE)
    all_rows = remote(here, ar_half, final, one_send, three_recv)
    most_rows = remote(here, ar_half.at[most], final.at[most], one_send, three_recv)

    if comm:

        def send_one(q):
            @pl.when(q != my_slice)
            def _():
                copy_one(q).start()

        loop(0, SLICES, send_one)

    def scatter(b, carry):
        sl = pl.ds(pl.multiple_of(b * block, block), block)
        chunk = part[:, sl]
        dg = None
        for deg in range(3):
            rws = slice(deg * width, (deg + 1) * width)
            one = radial[rws, sl] * dweight[rws, sl]
            dg = one if dg is None else dg + one
        dgm = jnp.concatenate([jnp.where(chunk == c, dg, 0.0).astype(BF16) for c in range(chunks)], axis=0)
        dtab[...] += mm_nt(one_src[:, sl], dgm)
        return carry

    lax.fori_loop(0, edges // block, scatter, 0)

    for c in range(chunks):
        dtab_out[c * CHUNK : (c + 1) * CHUNK, :] = dtab[:, c * width : (c + 1) * width].astype(BF16)
    returns = [
        to_peer(
            p,
            dtab_out.at[pl.ds(owned + p * slots, slots)],
            back.at[pl.ds(p * slots, slots)],
            back_send,
            back_recv,
            -1,
        )
        for p in range(6)
    ]
    for copy in returns:
        copy.start()

    if comm:

        @pl.when(owner)
        def _():
            all_one.wait_recv()
            total = ar_half[rows_of(my_slice), :].astype(F32)
            for s in range(1, group):
                total = total + got_one[s].astype(F32)
            got_two[plane] = total
            loop(1, planes, lambda s: copy_two(s).start())

    def sums(b, carry):
        sl = pl.ds(pl.multiple_of(b * 256, 256), 256)
        for deg in range(3):
            w = radial[deg * width : (deg + 1) * width, sl] * gathered[:, sl]
            for m in range(1, 9):
                if DEGREE[m] == deg:
                    d = dterms[m * width : (m + 1) * width, sl].astype(F32)
                    dharm[m - 1 : m, sl] = jnp.sum(w * d, axis=0, keepdims=True)
        return carry

    lax.fori_loop(0, edges // 256, sums, 0, unroll=2)

    if comm:

        @pl.when(owner)
        def _():
            all_two.wait_recv()
            total = got_two[0]
            for s in range(1, planes):
                total = total + got_two[s]
            half_three[...] = total.astype(BF16)
            loop(1, group, lambda s: copy_three(s).start())
            own = pltpu.make_async_copy(half_three, final.at[rows_of(my_slice)], own_sem)
            own.start()
            own.wait()

    dbas = mm(w1_both, dpre[...])
    ddist = jnp.sum((dbas[:8] + dbas[8:]) * dbasis[...], axis=0, keepdims=True)
    ux, uy, uz, inv = (geom[i : i + 1, :] for i in range(4))
    g1, g2, g3, g4, g5, g6, g7, g8 = (dharm[i : i + 1, :] for i in range(8))
    dx = r3 * g1 + r15 * (g4 * uy + g7 * uz + g8 * ux)
    dy = r3 * g2 + r15 * (g4 * ux + g5 * uz - g8 * uy)
    dz = r3 * g3 + r15 * (g5 * uy + g7 * ux) + (3.0 * r5) * (uz * g6)
    dd = ddist - (dx * ux + dy * uy + dz * uz) * inv
    force[0:1, :] = dx * inv + ux * dd
    force[1:2, :] = dy * inv + uy * dd
    force[2:3, :] = dz * inv + uz * dd

    for deg in range(3):
        hi, lo = mix_hl[deg]
        mix_t = jnp.concatenate([mm_nt(eye128, hi), mm_nt(eye128, lo)], axis=1).astype(BF16)
        for m in range(9):
            if DEGREE[m] == deg:
                out_t = mm(mix_t, jnp.concatenate([accb[m], accb[m]], axis=0)).astype(BF16)
                mixed[:, m * width : (m + 1) * width] = mm_nt(eye256, out_t).astype(BF16)
    stores = [
        pltpu.make_async_copy(a, b, out_sem.at[i])
        for i, (a, b) in enumerate(((mixed, mixed_far), (grad_feat, grad_feat_far), (force, force_far)))
    ]
    stores[0].start()
    stores[2].start()

    for copy in returns:
        if comm:
            copy.wait_recv()
        else:
            copy.wait()
    total = dtab[:, 0:width]
    for p in range(6):
        total = total + mm(picks(p), back[p * slots : (p + 1) * slots, :])
    grad_feat[...] = total
    stores[1].start()

    if comm:
        for copy in ghosts:
            copy.wait_send()
        for copy in returns:
            copy.wait_send()

        @pl.when(owner)
        def _():
            most_rows.wait_send()
            all_two.wait_send()
            loop(1, group, lambda s: copy_three(s).wait_send())
            most_rows.wait_recv()

        @pl.when(jnp.logical_not(owner))
        def _():
            all_rows.wait_send()
            all_rows.wait_recv()

    else:
        own = pltpu.make_async_copy(ar_half, final, own_sem)
        own.start()
        own.wait()
    for store in stores:
        store.wait()


def finish(mixed_in, feat_in, force_in, rows, mixed, grad_feat, force, grad_one, grad_two, grad_mix, sems):
    width = rows.shape[1]
    copies = [
        pltpu.make_async_copy(a, b, sems.at[i])
        for i, (a, b) in enumerate(((mixed_in, mixed), (feat_in, grad_feat), (force_in, force)))
    ]
    for copy in copies:
        copy.start()
    for deg in range(3):
        grad_mix[deg] = rows[deg * width : (deg + 1) * width, :].astype(F32)
    row = 3 * width
    for deg in range(3):
        grad_two[:, deg * width : (deg + 1) * width] = rows[row : row + 64, :].astype(F32)
        row += 64
    grad_one[...] = rows[row : row + 16, :].astype(F32)[0:8, 0:64]
    for copy in copies:
        copy.wait()


def on_device(
    nx,
    ny,
    block,
    features,
    edge_vec,
    edge_src,
    edge_dst,
    edge_count,
    send_gx,
    send_gy,
    w_one,
    w_two,
    mix,
    cotangent,
):
    owned, width = features.shape
    edges = edge_vec.shape[1]
    slots = send_gx.shape[1]
    hid = w_one.shape[1]
    rows = -(-(owned + 6 * slots) // CHUNK) * CHUNK
    chunks = rows // CHUNK
    group = PLANE_X * ny
    planes = max(nx // PLANE_X, 2)
    vmem = pl.BlockSpec(memory_space=pltpu.VMEM)
    far = pl.BlockSpec(memory_space=pl.ANY)
    dma = pltpu.SemaphoreType.DMA
    args = (
        features,
        edge_vec,
        edge_src.reshape(1, edges),
        edge_dst.reshape(1, edges),
        edge_count.reshape(1, 1),
        send_gx,
        send_gy,
        w_one,
        w_two,
        mix,
        cotangent,
    )
    shapes = (
        jax.ShapeDtypeStruct((owned, 9 * width), BF16),
        jax.ShapeDtypeStruct((owned, width), F32),
        jax.ShapeDtypeStruct((3, edges), F32),
    )
    scratch = [
        *(pltpu.VMEM(a.shape, a.dtype) for a in args),
        *(pltpu.VMEM(a.shape, a.dtype) for a in shapes),
        pltpu.VMEM((rows, width), BF16),
        pltpu.VMEM((6 * slots, width), BF16),
        pltpu.VMEM((rows, width), BF16),
        pltpu.VMEM((6 * slots, width), BF16),
        pltpu.VMEM((CHUNK, chunks * width), F32),
        pltpu.VMEM((9 * width, owned), F32),
        pltpu.VMEM((9 * width, owned), BF16),
        pltpu.VMEM((CHUNK, edges), BF16),
        pltpu.VMEM((owned, edges), BF16),
        pltpu.VMEM((3 * width, edges), F32),
        pltpu.VMEM((3 * width, edges), F32),
        pltpu.VMEM((9 * width, edges), BF16),
        pltpu.VMEM((hid, edges), F32),
        pltpu.VMEM((hid, edges), BF16),
        pltpu.VMEM((8, edges), F32),
        pltpu.VMEM((16, edges), BF16),
        pltpu.VMEM((8, edges), F32),
        pltpu.VMEM((8, edges), F32),
        pltpu.VMEM((1, edges), jnp.int32),
        pltpu.VMEM((8, edges), F32),
        pltpu.VMEM((hid, 3 * width), F32),
        pltpu.VMEM((hid, edges), BF16),
        pltpu.VMEM((width, edges), F32),
        pltpu.VMEM((SLICES * SLICE, width), BF16),
        pltpu.VMEM((group, SLICE, width), BF16),
        pltpu.VMEM((planes, SLICE, width), F32),
        pltpu.VMEM((SLICE, width), BF16),
        dma((6,)),
        dma((6,)),
        dma((6,)),
        dma((6,)),
        dma,
        dma,
        dma,
        dma,
        dma,
        dma,
        dma,
        dma((11,)),
        dma((3,)),
    ]
    params = {"vmem_limit_bytes": 60 * 1024 * 1024}
    if nx > 1:
        params.update(collective_id=0, has_side_effects=True)
    mixed, grad_feat, force, final = pl.pallas_call(
        functools.partial(kernel, nx, ny, block),
        out_shape=(*shapes, jax.ShapeDtypeStruct((SLICES * SLICE, width), BF16)),
        in_specs=[far] * 11,
        out_specs=(far,) * 4,
        scratch_shapes=scratch,
        compiler_params=pltpu.CompilerParams(**params),
        name="interaction",
    )(*args)
    return pl.pallas_call(
        finish,
        out_shape=(
            *shapes,
            jax.ShapeDtypeStruct(w_one.shape, F32),
            jax.ShapeDtypeStruct(w_two.shape, F32),
            jax.ShapeDtypeStruct(mix.shape, F32),
        ),
        in_specs=[vmem] * 4,
        out_specs=(far, far, far, vmem, vmem, vmem),
        scratch_shapes=[dma((3,))],
        name="finish",
    )(mixed, grad_feat, force, final)


def solution(mesh, block=2048):
    tiles = ("gx", "gy")
    return jax.shard_map(
        functools.partial(on_device, mesh.shape["gx"], mesh.shape["gy"], block),
        mesh=mesh,
        in_specs=(
            P(tiles, None),
            P(None, tiles),
            P(tiles),
            P(tiles),
            P(tiles),
            P(tiles, None),
            P(tiles, None),
            P(),
            P(),
            P(),
            P(tiles, None),
        ),
        out_specs=(
            P(tiles, None),
            P(tiles, None),
            P(None, tiles),
            P(),
            P(),
            P(),
        ),
        check_vma=False,
    )
```

```python
import functools
import math

import jax
import jax.numpy as jnp
from jax import lax
from jax.experimental import pallas as pl
from jax.experimental.pallas import tpu as pltpu
from jax.sharding import PartitionSpec as P

F32 = jnp.float32
BF16 = jnp.bfloat16
DEGREE = [0, 1, 1, 1, 2, 2, 2, 2, 2]
ROW_STEPS = [1, -1, 2, -2]
COLUMN_STEPS = [1, -1]
CHUNK = 256
SLICE = 32
SLICES = 19
PLANE_X = 4
SPREAD = 5
SPREAD_INVERSE = 13
NEAR_FIRST = (0, 1, 3, 2)
FAR_FIRST = (2, 1, 3, 0)


def mm(a, b):
    return jnp.dot(a, b, preferred_element_type=F32)


def mm_nt(a, b):
    return lax.dot_general(a, b, (((1,), (1,)), ((), ())), preferred_element_type=F32)


def eye(n):
    rows = lax.broadcasted_iota(jnp.int32, (n, n), 0)
    cols = lax.broadcasted_iota(jnp.int32, (n, n), 1)
    return jnp.where(rows == cols, 1.0, 0.0).astype(BF16)


def split(a):
    hi = a.astype(BF16)
    lo = (a - hi.astype(F32)).astype(BF16)
    return hi, lo


def kernel(
    nx,
    ny,
    block,
    *refs,
):
    inputs = refs[:11]
    mixed_far, grad_feat_far, force_far, final = refs[11:15]
    near = refs[15:26]
    (
        features,
        vec,
        src,
        dst,
        count,
        send_x,
        send_y,
        w_one,
        w_two,
        mix,
        cot,
    ) = near
    (
        mixed,
        grad_feat,
        force,
        table,
        outgoing,
        dtab_out,
        back,
        dtab,
        acc,
        dacc,
        one_src,
        one_dst,
        radial,
        dweight,
        dterms,
        dsilu,
        hidden,
        harm,
        basis2,
        dbasis,
        geom,
        part,
        dharm,
        dw_two,
        dpre,
        gathered,
        ar_half,
        got_one,
        got_two,
        half_three,
        ghost_send,
        ghost_recv,
        back_send,
        back_recv,
        one_send,
        one_recv,
        two_send,
        two_recv,
        three_send,
        three_recv,
        own_sem,
        in_sem,
        out_sem,
    ) = refs[26:]
    owned, width = features.shape
    edges = vec.shape[1]
    slots = send_x.shape[1]
    comm = nx > 1
    chunks = table.shape[0] // CHUNK
    me_x = lax.axis_index("gx")
    me_y = lax.axis_index("gy")
    factor = math.sqrt(owned / edges)
    group = PLANE_X * ny
    planes = nx // PLANE_X
    plane = lax.div(me_x, PLANE_X)
    member = lax.rem(me_x, PLANE_X) * ny + me_y
    my_slice = lax.rem(member * SPREAD_INVERSE, group)
    owner = my_slice < SLICES

    def loop(low, high, f):
        def step(s, c):
            f(s)
            return c

        lax.fori_loop(low, high, step, 0)

    def plane_loop(f, order):
        for step in order:
            column = lax.rem(lax.rem(me_x, PLANE_X) + step, PLANE_X) * ny
            loop(1 if step == 0 else 0, ny, lambda s: f(column + lax.rem(me_y + s, ny)))

    def in_plane(u):
        return {"gx": plane * PLANE_X + lax.div(u, ny), "gy": lax.rem(u, ny)}

    def along(s):
        return {"gx": lax.rem(me_x + s + nx, nx)}

    def across(s):
        return {"gy": lax.rem(me_y + s + ny, ny)}

    if comm:
        barrier = pltpu.get_barrier_semaphore()

        def greet(where):
            pl.semaphore_signal(barrier, inc=1, device_id=where, device_id_type=pl.DeviceIdType.MESH)

        for s in ROW_STEPS:
            greet(along(s))
        loop(1, planes, lambda s: greet(along(s * PLANE_X)))
        plane_loop(lambda u: greet(in_plane(u)), NEAR_FIRST)

    loads = [pltpu.make_async_copy(a, b, in_sem.at[i]) for i, (a, b) in enumerate(zip(inputs, near))]
    for i in (0, 5, 6, 10, 9, 8, 7, 1, 2, 3, 4):
        loads[i].start()

    def remote(where, source, target, send, recv):
        return pltpu.make_async_remote_copy(
            src_ref=source,
            dst_ref=target,
            send_sem=send,
            recv_sem=recv,
            device_id=where,
            device_id_type=pl.DeviceIdType.MESH,
        )

    def to_peer(p, source, target, sends, recvs, sign):
        where = along(sign * ROW_STEPS[p]) if p < 4 else across(sign * COLUMN_STEPS[p - 4])
        if not comm:
            return pltpu.make_async_copy(source, target, recvs.at[p])
        return remote(where, source, target, sends.at[p], recvs.at[p])

    eye128 = eye(128)
    for i in (0, 5, 6):
        loads[i].wait()
    feats = features[...]

    def picks(p):
        row = send_x[p : p + 1, :] if p < 4 else send_y[p - 4 : p - 3, :]
        rows = lax.broadcasted_iota(jnp.int32, (owned, slots), 0)
        return jnp.where(rows == row, 1.0, 0.0).astype(BF16)

    for p in range(6):
        outgoing[p * slots : (p + 1) * slots, :] = mm(picks(p).T, feats).astype(BF16)
    if comm:
        pl.semaphore_wait(barrier, group + planes + len(ROW_STEPS) - 2)
    ghosts = [
        to_peer(
            p,
            outgoing.at[pl.ds(p * slots, slots)],
            table.at[pl.ds(owned + p * slots, slots)],
            ghost_send,
            ghost_recv,
            1,
        )
        for p in range(6)
    ]
    for copy in ghosts:
        copy.start()

    dtab[...] = jnp.zeros_like(dtab)
    acc[...] = jnp.zeros_like(acc)
    dw_two[...] = jnp.zeros_like(dw_two)
    table[0:owned, :] = feats
    used = owned + 6 * slots
    table[used:, :] = jnp.zeros((table.shape[0] - used, width), BF16)

    for i in (7, 8, 9, 1, 2, 3, 4):
        loads[i].wait()
    w1h, w1l = split(w_one[...])
    w1h = w1h.astype(F32)
    w1l = w1l.astype(F32)
    w1_both = jnp.concatenate([w1h, w1l], axis=0).astype(BF16)
    w1_stack = jnp.concatenate([w1h, w1h, w1l, jnp.zeros_like(w1l)], axis=0).astype(BF16)
    w1_t = mm_nt(eye128[:64, :64], w1_stack).astype(BF16)
    w2h, w2l = split(w_two[...])
    w2_both = jnp.concatenate([w2h, w2l], axis=0)
    w2_stack = jnp.concatenate([w2h, w2h, w2l], axis=0)
    w2_t = jnp.concatenate(
        [w2_stack[:, deg * width : (deg + 1) * width].T for deg in range(3)],
        axis=0,
    )
    mix_hl = [split(mix[deg]) for deg in range(3)]
    loads[10].wait()
    for m in range(9):
        hi, lo = mix_hl[DEGREE[m]]
        cot_m = cot[:, m * width : (m + 1) * width]
        both = mm_nt(jnp.concatenate([hi, lo], axis=1), jnp.concatenate([cot_m, cot_m], axis=1))
        dacc[m * width : (m + 1) * width, :] = (both * factor).astype(BF16)

    live_count = count[...]
    r3 = math.sqrt(3.0)
    r5 = math.sqrt(5.0)
    r15 = math.sqrt(15.0)
    pi = math.pi

    def part_one(block):
        sl = pl.ds(0, block)
        index = src[:, sl]
        chunk = lax.shift_right_logical(index, 8)
        part[:, sl] = chunk
        rows = lax.broadcasted_iota(jnp.int32, (CHUNK, block), 0)
        one_src[:, sl] = jnp.where(rows == index - chunk * CHUNK, 1.0, 0.0).astype(BF16)
        one_dst[:, sl] = jnp.where(rows == dst[:, sl], 1.0, 0.0).astype(BF16)
        dall = mm(dacc[...], one_dst[:, sl])
        dterms[:, sl] = dall.astype(BF16)

        v = vec[:, sl]
        x, y, z = v[0:1], v[1:2], v[2:3]
        dist = jnp.sqrt(x * x + y * y + z * z + 0.25)
        inv = 1.0 / dist
        ratio = dist * (1.0 / 5.0)
        ra2 = ratio * ratio
        ra5 = ra2 * ra2 * ratio
        env = 1.0 / (1.0 + ra5 * ratio)
        ux, uy, uz = x * inv, y * inv, z * inv
        geom[0:1, sl] = ux
        geom[1:2, sl] = uy
        geom[2:3, sl] = uz
        geom[3:4, sl] = inv
        hs = [
            r3 * ux,
            r3 * uy,
            r3 * uz,
            r15 * ux * uy,
            r15 * uy * uz,
            0.5 * r5 * (3.0 * uz * uz - 1.0),
            r15 * ux * uz,
            0.5 * r15 * (ux * ux - uy * uy),
        ]
        for i in range(8):
            harm[i : i + 1, sl] = hs[i]
        k = (lax.broadcasted_iota(jnp.int32, (8, block), 0) + 1).astype(F32)
        t = k * ratio
        n = jnp.floor(t + 0.5)
        r = t - n
        sgn = 1.0 - 2.0 * (n - 2.0 * jnp.floor(n * 0.5))
        q = r * r
        s_pi = pi**9 / 362880.0 - q * (pi**11 / 39916800.0)
        s_pi = pi**7 / 5040.0 - q * s_pi
        s_pi = pi**5 / 120.0 - q * s_pi
        s_pi = pi**3 / 6.0 - q * s_pi
        s_pi = r * (pi - q * s_pi)
        c_pi = pi**10 / 3628800.0 - q * (pi**12 / 479001600.0)
        c_pi = pi**8 / 40320.0 - q * c_pi
        c_pi = pi**6 / 720.0 - q * c_pi
        c_pi = pi**4 / 24.0 - q * c_pi
        c_pi = pi**2 / 2.0 - q * c_pi
        c_pi = 1.0 - q * c_pi
        amp = sgn * (inv * env)
        bas = s_pi * amp
        dbasis[:, sl] = c_pi * amp * (k * (pi / 5.0)) - bas * (inv + (6.0 / 5.0) * (env * ra5))
        bh = bas.astype(BF16).astype(F32)
        bl = bas - bh
        basis2[:, sl] = jnp.concatenate([bh, bl], axis=0).astype(BF16)
        bstack = jnp.concatenate([bh, bl, bh, jnp.zeros_like(bh)], axis=0).astype(BF16)
        pre = mm(w1_t, bstack)
        spot = lax.broadcasted_iota(jnp.int32, (1, block), 1)
        live = jnp.where(spot < live_count, 1.0, 0.0)
        sig = 1.0 / (1.0 + jnp.exp(-pre))
        sig_live = sig * live
        hid = pre * sig_live
        dsilu[:, sl] = sig_live * (1.0 + pre * (1.0 - sig))
        hh, hl = split(hid)
        hidden[:, sl] = hh
        radial[:, sl] = mm(w2_t, jnp.concatenate([hh, hl, hh], axis=0))

        for deg, ms in enumerate(((0,), (1, 2, 3), (4, 5, 6, 7, 8))):
            total = None
            for m in ms:
                term = dall[m * width : (m + 1) * width]
                if m > 0:
                    term = term * hs[m - 1]
                total = term if total is None else total + term
            dweight[deg * width : (deg + 1) * width, sl] = total

    part_one(edges)

    for copy in ghosts:
        if comm:
            copy.wait_recv()
        else:
            copy.wait()
    table_t = jnp.concatenate(
        [table[c * CHUNK : (c + 1) * CHUNK, :].T for c in range(chunks)], axis=0
    )

    def gather(b):
        sl = pl.ds(pl.multiple_of(b * block, block), block)
        chunk = part[:, sl]
        got = mm(table_t, one_src[:, sl])
        g = got[0:width]
        for c in range(1, chunks):
            g = jnp.where(chunk == c, got[c * width : (c + 1) * width], g)
        gathered[:, sl] = g

    def part_two(b, carry):
        sl = pl.ds(pl.multiple_of(b * block, block), block)
        gather(b)
        g = gathered[:, sl]
        drad = jnp.concatenate(
            [(dweight[deg * width : (deg + 1) * width, sl] * g).astype(BF16) for deg in range(3)], axis=0
        )
        weighted = [radial[deg * width : (deg + 1) * width, sl] * g for deg in range(3)]
        terms = [weighted[0].astype(BF16)]
        for m in range(1, 9):
            terms.append((weighted[DEGREE[m]] * harm[m - 1 : m, sl]).astype(BF16))
        dhid = mm(w2_both, drad)
        dw_two[...] += mm_nt(hidden[:, sl], drad)
        acc[...] += (mm_nt(jnp.concatenate(terms, axis=0), one_dst[:, sl]))
        dpre[:, sl] = ((dhid[:64] + dhid[64:]) * dsilu[:, sl]).astype(BF16)
        return carry

    lax.fori_loop(0, edges // block, part_two, 0)
    dw_one = mm_nt(basis2[...], dpre[...])

    accb = [(acc[m * width : (m + 1) * width, :] * factor).astype(BF16) for m in range(9)]
    for deg in range(3):
        total = None
        for m in range(9):
            if DEGREE[m] == deg:
                one = mm(accb[m], cot[:, m * width : (m + 1) * width])
                total = one if total is None else total + one
        ar_half[deg * width : (deg + 1) * width, :] = total.astype(BF16)
    row = 3 * width
    for deg in range(3):
        ar_half[row : row + 64, :] = dw_two[:, deg * width : (deg + 1) * width].astype(BF16)
        row += 64
    tail = jnp.concatenate([dw_one[0:8, :] + dw_one[8:16, :], jnp.zeros((8, 64), F32)], axis=0)
    tail = jnp.concatenate([tail, jnp.zeros((16, 64), F32)], axis=1)
    ar_half[row : row + 16, :] = tail.astype(BF16)
    ar_half[row + 16 :, :] = jnp.zeros((ar_half.shape[0] - row - 16, width), BF16)

    def rows_of(q):
        return pl.ds(pl.multiple_of(q * SLICE, SLICE), SLICE)

    def copy_one(u, q):
        slot = lax.rem(member - u + group, group)
        return remote(in_plane(u), ar_half.at[rows_of(q)], got_one.at[slot], one_send, one_recv)

    def copy_two(s):
        return remote(along(s * PLANE_X), got_two.at[plane], got_two.at[plane], two_send, two_recv)

    def copy_three(u):
        return remote(in_plane(u), half_three, final.at[rows_of(my_slice)], three_send, three_recv)

    here = {"gx": me_x, "gy": me_y}
    all_one = remote(here, got_one.at[pl.ds(1, group - 1)], got_one.at[pl.ds(1, group - 1)], one_send, one_recv)
    all_two = remote(here, got_two.at[pl.ds(1, planes - 1)], got_two.at[pl.ds(1, planes - 1)], two_send, two_recv)
    most = pl.ds(0, (SLICES - 1) * SLICE)
    all_rows = remote(here, ar_half, final, one_send, three_recv)
    most_rows = remote(here, ar_half.at[most], final.at[most], one_send, three_recv)

    if comm:

        def send_one(u):
            q = lax.rem(u * SPREAD_INVERSE, group)

            @pl.when(q < SLICES)
            def _():
                copy_one(u, q).start()

        plane_loop(send_one, FAR_FIRST)

    def scatter(b, carry):
        sl = pl.ds(pl.multiple_of(b * block, block), block)
        chunk = part[:, sl]
        dg = None
        for deg in range(3):
            rws = slice(deg * width, (deg + 1) * width)
            one = radial[rws, sl] * dweight[rws, sl]
            dg = one if dg is None else dg + one
        dgm = jnp.concatenate([jnp.where(chunk == c, dg, 0.0).astype(BF16) for c in range(chunks)], axis=0)
        dtab[...] += mm_nt(one_src[:, sl], dgm)
        return carry

    lax.fori_loop(0, edges // block, scatter, 0)

    for c in range(chunks):
        dtab_out[c * CHUNK : (c + 1) * CHUNK, :] = dtab[:, c * width : (c + 1) * width].astype(BF16)
    returns = [
        to_peer(
            p,
            dtab_out.at[pl.ds(owned + p * slots, slots)],
            back.at[pl.ds(p * slots, slots)],
            back_send,
            back_recv,
            -1,
        )
        for p in range(6)
    ]
    for copy in returns:
        copy.start()

    if comm:

        @pl.when(owner)
        def _():
            all_one.wait_recv()
            total = ar_half[rows_of(my_slice), :].astype(F32)
            for s in range(1, group):
                total = total + got_one[s].astype(F32)
            got_two[plane] = total.astype(BF16)
            loop(1, planes, lambda s: copy_two(s).start())

    def sums(b, carry):
        sl = pl.ds(pl.multiple_of(b * 256, 256), 256)
        for deg in range(3):
            w = radial[deg * width : (deg + 1) * width, sl] * gathered[:, sl]
            for m in range(1, 9):
                if DEGREE[m] == deg:
                    d = dterms[m * width : (m + 1) * width, sl].astype(F32)
                    dharm[m - 1 : m, sl] = jnp.sum(w * d, axis=0, keepdims=True)
        return carry

    lax.fori_loop(0, edges // 256, sums, 0, unroll=2)

    if comm:

        @pl.when(owner)
        def _():
            all_two.wait_recv()
            total = got_two[0].astype(F32)
            for s in range(1, planes):
                total = total + got_two[s].astype(F32)
            half_three[...] = total.astype(BF16)
            plane_loop(lambda u: copy_three(u).start(), FAR_FIRST)
            own = pltpu.make_async_copy(half_three, final.at[rows_of(my_slice)], own_sem)
            own.start()
            own.wait()

    dbas = mm(w1_both, dpre[...])
    ddist = jnp.sum((dbas[:8] + dbas[8:]) * dbasis[...], axis=0, keepdims=True)
    ux, uy, uz, inv = (geom[i : i + 1, :] for i in range(4))
    g1, g2, g3, g4, g5, g6, g7, g8 = (dharm[i : i + 1, :] for i in range(8))
    dx = r3 * g1 + r15 * (g4 * uy + g7 * uz + g8 * ux)
    dy = r3 * g2 + r15 * (g4 * ux + g5 * uz - g8 * uy)
    dz = r3 * g3 + r15 * (g5 * uy + g7 * ux) + (3.0 * r5) * (uz * g6)
    dd = ddist - (dx * ux + dy * uy + dz * uz) * inv
    force[0:1, :] = dx * inv + ux * dd
    force[1:2, :] = dy * inv + uy * dd
    force[2:3, :] = dz * inv + uz * dd

    for deg in range(3):
        hi, lo = mix_hl[deg]
        mix_t = jnp.concatenate([mm_nt(eye128, hi), mm_nt(eye128, lo)], axis=1).astype(BF16)
        for m in range(9):
            if DEGREE[m] == deg:
                out_t = mm(mix_t, jnp.concatenate([accb[m], accb[m]], axis=0)).astype(BF16)
                mixed[:, m * width : (m + 1) * width] = out_t.T
    stores = [
        pltpu.make_async_copy(a, b, out_sem.at[i])
        for i, (a, b) in enumerate(((mixed, mixed_far), (grad_feat, grad_feat_far), (force, force_far)))
    ]
    stores[0].start()
    stores[2].start()

    for copy in returns:
        if comm:
            copy.wait_recv()
        else:
            copy.wait()
    total = dtab[:, 0:width]
    for p in range(6):
        total = total + mm(picks(p), back[p * slots : (p + 1) * slots, :])
    grad_feat[...] = total
    stores[1].start()

    if comm:
        for copy in ghosts:
            copy.wait_send()
        for copy in returns:
            copy.wait_send()

        @pl.when(owner)
        def _():
            most_rows.wait_send()
            all_two.wait_send()
            loop(1, group, lambda s: copy_three(member).wait_send())
            most_rows.wait_recv()

        @pl.when(jnp.logical_not(owner))
        def _():
            all_rows.wait_send()
            all_rows.wait_recv()

    else:
        own = pltpu.make_async_copy(ar_half, final, own_sem)
        own.start()
        own.wait()
    for store in stores:
        store.wait()


def finish(mixed_in, feat_in, force_in, rows, mixed, grad_feat, force, grad_one, grad_two, grad_mix, sems):
    width = rows.shape[1]
    copies = [
        pltpu.make_async_copy(a, b, sems.at[i])
        for i, (a, b) in enumerate(((mixed_in, mixed), (feat_in, grad_feat), (force_in, force)))
    ]
    for copy in copies:
        copy.start()
    for deg in range(3):
        grad_mix[deg] = rows[deg * width : (deg + 1) * width, :].astype(F32)
    row = 3 * width
    for deg in range(3):
        grad_two[:, deg * width : (deg + 1) * width] = rows[row : row + 64, :].astype(F32)
        row += 64
    grad_one[...] = rows[row : row + 16, :].astype(F32)[0:8, 0:64]
    for copy in copies:
        copy.wait()


def on_device(
    nx,
    ny,
    block,
    features,
    edge_vec,
    edge_src,
    edge_dst,
    edge_count,
    send_gx,
    send_gy,
    w_one,
    w_two,
    mix,
    cotangent,
):
    owned, width = features.shape
    edges = edge_vec.shape[1]
    slots = send_gx.shape[1]
    hid = w_one.shape[1]
    rows = -(-(owned + 6 * slots) // CHUNK) * CHUNK
    chunks = rows // CHUNK
    group = PLANE_X * ny
    planes = max(nx // PLANE_X, 2)
    vmem = pl.BlockSpec(memory_space=pltpu.VMEM)
    far = pl.BlockSpec(memory_space=pl.ANY)
    dma = pltpu.SemaphoreType.DMA
    args = (
        features,
        edge_vec,
        edge_src.reshape(1, edges),
        edge_dst.reshape(1, edges),
        edge_count.reshape(1, 1),
        send_gx,
        send_gy,
        w_one,
        w_two,
        mix,
        cotangent,
    )
    shapes = (
        jax.ShapeDtypeStruct((owned, 9 * width), BF16),
        jax.ShapeDtypeStruct((owned, width), F32),
        jax.ShapeDtypeStruct((3, edges), F32),
    )
    scratch = [
        *(pltpu.VMEM(a.shape, a.dtype) for a in args),
        *(pltpu.VMEM(a.shape, a.dtype) for a in shapes),
        pltpu.VMEM((rows, width), BF16),
        pltpu.VMEM((6 * slots, width), BF16),
        pltpu.VMEM((rows, width), BF16),
        pltpu.VMEM((6 * slots, width), BF16),
        pltpu.VMEM((CHUNK, chunks * width), F32),
        pltpu.VMEM((9 * width, owned), F32),
        pltpu.VMEM((9 * width, owned), BF16),
        pltpu.VMEM((CHUNK, edges), BF16),
        pltpu.VMEM((owned, edges), BF16),
        pltpu.VMEM((3 * width, edges), F32),
        pltpu.VMEM((3 * width, edges), F32),
        pltpu.VMEM((9 * width, edges), BF16),
        pltpu.VMEM((hid, edges), F32),
        pltpu.VMEM((hid, edges), BF16),
        pltpu.VMEM((8, edges), F32),
        pltpu.VMEM((16, edges), BF16),
        pltpu.VMEM((8, edges), F32),
        pltpu.VMEM((8, edges), F32),
        pltpu.VMEM((1, edges), jnp.int32),
        pltpu.VMEM((8, edges), F32),
        pltpu.VMEM((hid, 3 * width), F32),
        pltpu.VMEM((hid, edges), BF16),
        pltpu.VMEM((width, edges), F32),
        pltpu.VMEM((SLICES * SLICE, width), BF16),
        pltpu.VMEM((group, SLICE, width), BF16),
        pltpu.VMEM((planes, SLICE, width), BF16),
        pltpu.VMEM((SLICE, width), BF16),
        dma((6,)),
        dma((6,)),
        dma((6,)),
        dma((6,)),
        dma,
        dma,
        dma,
        dma,
        dma,
        dma,
        dma,
        dma((11,)),
        dma((3,)),
    ]
    params = {"vmem_limit_bytes": 60 * 1024 * 1024}
    if nx > 1:
        params.update(collective_id=0, has_side_effects=True)
    mixed, grad_feat, force, final = pl.pallas_call(
        functools.partial(kernel, nx, ny, block),
        out_shape=(*shapes, jax.ShapeDtypeStruct((SLICES * SLICE, width), BF16)),
        in_specs=[far] * 11,
        out_specs=(far,) * 4,
        scratch_shapes=scratch,
        compiler_params=pltpu.CompilerParams(**params),
        name="interaction",
    )(*args)
    return pl.pallas_call(
        finish,
        out_shape=(
            *shapes,
            jax.ShapeDtypeStruct(w_one.shape, F32),
            jax.ShapeDtypeStruct(w_two.shape, F32),
            jax.ShapeDtypeStruct(mix.shape, F32),
        ),
        in_specs=[vmem] * 4,
        out_specs=(far, far, far, vmem, vmem, vmem),
        scratch_shapes=[dma((3,))],
        name="finish",
    )(mixed, grad_feat, force, final)


def solution(mesh, block=2048):
    tiles = ("gx", "gy")
    return jax.shard_map(
        functools.partial(on_device, mesh.shape["gx"], mesh.shape["gy"], block),
        mesh=mesh,
        in_specs=(
            P(tiles, None),
            P(None, tiles),
            P(tiles),
            P(tiles),
            P(tiles),
            P(tiles, None),
            P(tiles, None),
            P(),
            P(),
            P(),
            P(tiles, None),
        ),
        out_specs=(
            P(tiles, None),
            P(tiles, None),
            P(None, tiles),
            P(),
            P(),
            P(),
        ),
        check_vma=False,
    )
```

```python
import functools
import math

import jax
import jax.numpy as jnp
from jax import lax
from jax.experimental import pallas as pl
from jax.experimental.pallas import tpu as pltpu
from jax.sharding import PartitionSpec as P

F32 = jnp.float32
BF16 = jnp.bfloat16
DEGREE = [0, 1, 1, 1, 2, 2, 2, 2, 2]
ROW_STEPS = [1, -1, 2, -2]
COLUMN_STEPS = [1, -1]
CHUNK = 256
SLICE = 32
SLICES = 19
PLANE_X = 4
SPREAD = 5
SPREAD_INVERSE = 13
NEAR_FIRST = (0, 1, 3, 2)
FAR_FIRST = (2, 1, 3, 0)


def mm(a, b):
    return jnp.dot(a, b, preferred_element_type=F32)


def mm_nt(a, b):
    return lax.dot_general(a, b, (((1,), (1,)), ((), ())), preferred_element_type=F32)


def eye(n):
    rows = lax.broadcasted_iota(jnp.int32, (n, n), 0)
    cols = lax.broadcasted_iota(jnp.int32, (n, n), 1)
    return jnp.where(rows == cols, 1.0, 0.0).astype(BF16)


def split(a):
    hi = a.astype(BF16)
    lo = (a - hi.astype(F32)).astype(BF16)
    return hi, lo


def kernel(
    nx,
    ny,
    block,
    *refs,
):
    inputs = refs[:11]
    mixed_far, grad_feat_far, force_far, final = refs[11:15]
    near = refs[15:26]
    (
        features,
        vec,
        src,
        dst,
        count,
        send_x,
        send_y,
        w_one,
        w_two,
        mix,
        cot,
    ) = near
    (
        mixed,
        grad_feat,
        force,
        table,
        outgoing,
        dtab_out,
        back,
        dtab,
        acc,
        dacc,
        one_src,
        one_dst,
        radial,
        dweight,
        dterms,
        dsilu,
        hidden,
        harm,
        basis2,
        dbasis,
        geom,
        part,
        dharm,
        dw_two,
        dpre,
        gathered,
        ar_half,
        got_one,
        got_two,
        half_three,
        ghost_send,
        ghost_recv,
        back_send,
        back_recv,
        one_send,
        one_recv,
        two_send,
        two_recv,
        three_send,
        three_recv,
        own_sem,
        in_sem,
        out_sem,
    ) = refs[26:]
    owned, width = features.shape
    edges = vec.shape[1]
    slots = send_x.shape[1]
    comm = nx > 1
    chunks = table.shape[0] // CHUNK
    me_x = lax.axis_index("gx")
    me_y = lax.axis_index("gy")
    factor = math.sqrt(owned / edges)
    group = PLANE_X * ny
    planes = nx // PLANE_X
    plane = lax.div(me_x, PLANE_X)
    member = lax.rem(me_x, PLANE_X) * ny + me_y
    my_slice = lax.rem(member * SPREAD_INVERSE, group)
    owner = my_slice < SLICES

    def loop(low, high, f):
        def step(s, c):
            f(s)
            return c

        lax.fori_loop(low, high, step, 0)

    def plane_loop(f, order):
        for step in order:
            column = lax.rem(lax.rem(me_x, PLANE_X) + step, PLANE_X) * ny
            loop(1 if step == 0 else 0, ny, lambda s: f(column + lax.rem(me_y + s, ny)))

    def in_plane(u):
        return {"gx": plane * PLANE_X + lax.div(u, ny), "gy": lax.rem(u, ny)}

    def along(s):
        return {"gx": lax.rem(me_x + s + nx, nx)}

    def across(s):
        return {"gy": lax.rem(me_y + s + ny, ny)}

    if comm:
        barrier = pltpu.get_barrier_semaphore()

        def greet(where):
            pl.semaphore_signal(barrier, inc=1, device_id=where, device_id_type=pl.DeviceIdType.MESH)

        for s in ROW_STEPS:
            greet(along(s))
        loop(1, planes, lambda s: greet(along(s * PLANE_X)))
        plane_loop(lambda u: greet(in_plane(u)), NEAR_FIRST)

    loads = [pltpu.make_async_copy(a, b, in_sem.at[i]) for i, (a, b) in enumerate(zip(inputs, near))]
    for i in (0, 5, 6, 10, 9, 8, 7, 1, 2, 3, 4):
        loads[i].start()

    def remote(where, source, target, send, recv):
        return pltpu.make_async_remote_copy(
            src_ref=source,
            dst_ref=target,
            send_sem=send,
            recv_sem=recv,
            device_id=where,
            device_id_type=pl.DeviceIdType.MESH,
        )

    def to_peer(p, source, target, sends, recvs, sign):
        where = along(sign * ROW_STEPS[p]) if p < 4 else across(sign * COLUMN_STEPS[p - 4])
        if not comm:
            return pltpu.make_async_copy(source, target, recvs.at[p])
        return remote(where, source, target, sends.at[p], recvs.at[p])

    eye128 = eye(128)
    for i in (0, 5, 6):
        loads[i].wait()
    feats = features[...]

    def picks(p):
        row = send_x[p : p + 1, :] if p < 4 else send_y[p - 4 : p - 3, :]
        rows = lax.broadcasted_iota(jnp.int32, (owned, slots), 0)
        return jnp.where(rows == row, 1.0, 0.0).astype(BF16)

    for p in range(6):
        outgoing[p * slots : (p + 1) * slots, :] = mm(picks(p).T, feats).astype(BF16)
    if comm:
        pl.semaphore_wait(barrier, group + planes + len(ROW_STEPS) - 2)
    ghosts = [
        to_peer(
            p,
            outgoing.at[pl.ds(p * slots, slots)],
            table.at[pl.ds(owned + p * slots, slots)],
            ghost_send,
            ghost_recv,
            1,
        )
        for p in range(6)
    ]
    for copy in ghosts:
        copy.start()

    dtab[...] = jnp.zeros_like(dtab)
    acc[...] = jnp.zeros_like(acc)
    dw_two[...] = jnp.zeros_like(dw_two)
    table[0:owned, :] = feats
    used = owned + 6 * slots
    table[used:, :] = jnp.zeros((table.shape[0] - used, width), BF16)

    for i in (7, 8, 9, 1, 2, 3, 4):
        loads[i].wait()
    w1h, w1l = split(w_one[...])
    w1h = w1h.astype(F32)
    w1l = w1l.astype(F32)
    w1_both = jnp.concatenate([w1h, w1l], axis=0).astype(BF16)
    w1_stack = jnp.concatenate([w1h, w1h, w1l, jnp.zeros_like(w1l)], axis=0).astype(BF16)
    w1_t = mm_nt(eye128[:64, :64], w1_stack).astype(BF16)
    w2h, w2l = split(w_two[...])
    w2_both = jnp.concatenate([w2h, w2l], axis=0)
    w2_stack = jnp.concatenate([w2h, w2h, w2l], axis=0)
    w2_t = jnp.concatenate(
        [w2_stack[:, deg * width : (deg + 1) * width].T for deg in range(3)],
        axis=0,
    )
    mix_hl = [split(mix[deg]) for deg in range(3)]
    loads[10].wait()
    for m in range(9):
        hi, lo = mix_hl[DEGREE[m]]
        cot_m = cot[:, m * width : (m + 1) * width]
        both = mm_nt(jnp.concatenate([hi, lo], axis=1), jnp.concatenate([cot_m, cot_m], axis=1))
        dacc[m * width : (m + 1) * width, :] = (both * factor).astype(BF16)

    live_count = count[...]
    r3 = math.sqrt(3.0)
    r5 = math.sqrt(5.0)
    r15 = math.sqrt(15.0)
    pi = math.pi

    def part_one(block):
        sl = pl.ds(0, block)
        index = src[:, sl]
        chunk = lax.shift_right_logical(index, 8)
        part[:, sl] = chunk
        rows = lax.broadcasted_iota(jnp.int32, (CHUNK, block), 0)
        one_src[:, sl] = jnp.where(rows == index - chunk * CHUNK, 1.0, 0.0).astype(BF16)
        one_dst[:, sl] = jnp.where(rows == dst[:, sl], 1.0, 0.0).astype(BF16)
        dall = mm(dacc[...], one_dst[:, sl])
        dterms[:, sl] = dall.astype(BF16)

        v = vec[:, sl]
        x, y, z = v[0:1], v[1:2], v[2:3]
        dist = jnp.sqrt(x * x + y * y + z * z + 0.25)
        inv = 1.0 / dist
        ratio = dist * (1.0 / 5.0)
        ra2 = ratio * ratio
        ra5 = ra2 * ra2 * ratio
        env = 1.0 / (1.0 + ra5 * ratio)
        ux, uy, uz = x * inv, y * inv, z * inv
        geom[0:1, sl] = ux
        geom[1:2, sl] = uy
        geom[2:3, sl] = uz
        geom[3:4, sl] = inv
        hs = [
            r3 * ux,
            r3 * uy,
            r3 * uz,
            r15 * ux * uy,
            r15 * uy * uz,
            0.5 * r5 * (3.0 * uz * uz - 1.0),
            r15 * ux * uz,
            0.5 * r15 * (ux * ux - uy * uy),
        ]
        for i in range(8):
            harm[i : i + 1, sl] = hs[i]
        k = (lax.broadcasted_iota(jnp.int32, (8, block), 0) + 1).astype(F32)
        t = k * ratio
        n = jnp.floor(t + 0.5)
        r = t - n
        sgn = 1.0 - 2.0 * (n - 2.0 * jnp.floor(n * 0.5))
        q = r * r
        s_pi = pi**9 / 362880.0 - q * (pi**11 / 39916800.0)
        s_pi = pi**7 / 5040.0 - q * s_pi
        s_pi = pi**5 / 120.0 - q * s_pi
        s_pi = pi**3 / 6.0 - q * s_pi
        s_pi = r * (pi - q * s_pi)
        c_pi = pi**10 / 3628800.0 - q * (pi**12 / 479001600.0)
        c_pi = pi**8 / 40320.0 - q * c_pi
        c_pi = pi**6 / 720.0 - q * c_pi
        c_pi = pi**4 / 24.0 - q * c_pi
        c_pi = pi**2 / 2.0 - q * c_pi
        c_pi = 1.0 - q * c_pi
        amp = sgn * (inv * env)
        bas = s_pi * amp
        dbasis[:, sl] = c_pi * amp * (k * (pi / 5.0)) - bas * (inv + (6.0 / 5.0) * (env * ra5))
        bh = bas.astype(BF16).astype(F32)
        bl = bas - bh
        basis2[:, sl] = jnp.concatenate([bh, bl], axis=0).astype(BF16)
        bstack = jnp.concatenate([bh, bl, bh, jnp.zeros_like(bh)], axis=0).astype(BF16)
        pre = mm(w1_t, bstack)
        spot = lax.broadcasted_iota(jnp.int32, (1, block), 1)
        live = jnp.where(spot < live_count, 1.0, 0.0)
        sig = 1.0 / (1.0 + jnp.exp(-pre))
        sig_live = sig * live
        hid = pre * sig_live
        dsilu[:, sl] = sig_live * (1.0 + pre * (1.0 - sig))
        hh, hl = split(hid)
        hidden[:, sl] = hh
        radial[:, sl] = mm(w2_t, jnp.concatenate([hh, hl, hh], axis=0))

        for deg, ms in enumerate(((0,), (1, 2, 3), (4, 5, 6, 7, 8))):
            total = None
            for m in ms:
                term = dall[m * width : (m + 1) * width]
                if m > 0:
                    term = term * hs[m - 1]
                total = term if total is None else total + term
            dweight[deg * width : (deg + 1) * width, sl] = total

    part_one(edges)

    for copy in ghosts:
        if comm:
            copy.wait_recv()
        else:
            copy.wait()
    table_t = jnp.concatenate(
        [table[c * CHUNK : (c + 1) * CHUNK, :].T for c in range(chunks)], axis=0
    )

    def gather(b):
        sl = pl.ds(pl.multiple_of(b * block, block), block)
        chunk = part[:, sl]
        got = mm(table_t, one_src[:, sl])
        g = got[0:width]
        for c in range(1, chunks):
            g = jnp.where(chunk == c, got[c * width : (c + 1) * width], g)
        gathered[:, sl] = g

    def part_two(b, carry):
        sl = pl.ds(pl.multiple_of(b * block, block), block)
        gather(b)
        g = gathered[:, sl]
        drad = jnp.concatenate(
            [(dweight[deg * width : (deg + 1) * width, sl] * g).astype(BF16) for deg in range(3)], axis=0
        )
        weighted = [radial[deg * width : (deg + 1) * width, sl] * g for deg in range(3)]
        terms = [weighted[0].astype(BF16)]
        for m in range(1, 9):
            terms.append((weighted[DEGREE[m]] * harm[m - 1 : m, sl]).astype(BF16))
        dhid = mm(w2_both, drad)
        dw_two[...] += mm_nt(hidden[:, sl], drad)
        acc[...] += (mm_nt(jnp.concatenate(terms, axis=0), one_dst[:, sl]))
        dpre[:, sl] = ((dhid[:64] + dhid[64:]) * dsilu[:, sl]).astype(BF16)
        return carry

    lax.fori_loop(0, edges // block, part_two, 0)
    dw_one = mm_nt(basis2[...], dpre[...])

    accb = [(acc[m * width : (m + 1) * width, :] * factor).astype(BF16) for m in range(9)]
    for deg in range(3):
        total = None
        for m in range(9):
            if DEGREE[m] == deg:
                one = mm(accb[m], cot[:, m * width : (m + 1) * width])
                total = one if total is None else total + one
        ar_half[deg * width : (deg + 1) * width, :] = total.astype(BF16)
    row = 3 * width
    for deg in range(3):
        ar_half[row : row + 64, :] = dw_two[:, deg * width : (deg + 1) * width].astype(BF16)
        row += 64
    tail = jnp.concatenate([dw_one[0:8, :] + dw_one[8:16, :], jnp.zeros((8, 64), F32)], axis=0)
    tail = jnp.concatenate([tail, jnp.zeros((16, 64), F32)], axis=1)
    ar_half[row : row + 16, :] = tail.astype(BF16)
    ar_half[row + 16 :, :] = jnp.zeros((ar_half.shape[0] - row - 16, width), BF16)

    def rows_of(q):
        return pl.ds(pl.multiple_of(q * SLICE, SLICE), SLICE)

    def copy_one(u, q):
        slot = lax.rem(member - u + group, group)
        return remote(in_plane(u), ar_half.at[rows_of(q)], got_one.at[slot], one_send, one_recv)

    def copy_two(s):
        return remote(along(s * PLANE_X), got_two.at[plane], got_two.at[plane], two_send, two_recv)

    def copy_three(u):
        return remote(in_plane(u), half_three, final.at[rows_of(my_slice)], three_send, three_recv)

    here = {"gx": me_x, "gy": me_y}
    all_one = remote(here, got_one.at[pl.ds(1, group - 1)], got_one.at[pl.ds(1, group - 1)], one_send, one_recv)
    all_two = remote(here, got_two.at[pl.ds(1, planes - 1)], got_two.at[pl.ds(1, planes - 1)], two_send, two_recv)
    most = pl.ds(0, (SLICES - 1) * SLICE)
    all_rows = remote(here, ar_half, final, one_send, three_recv)
    most_rows = remote(here, ar_half.at[most], final.at[most], one_send, three_recv)

    if comm:

        def send_one(u):
            q = lax.rem(u * SPREAD_INVERSE, group)

            @pl.when(q < SLICES)
            def _():
                copy_one(u, q).start()

        plane_loop(send_one, FAR_FIRST)

    def scatter(b, carry):
        sl = pl.ds(pl.multiple_of(b * block, block), block)
        chunk = part[:, sl]
        dg = None
        for deg in range(3):
            rws = slice(deg * width, (deg + 1) * width)
            one = radial[rws, sl] * dweight[rws, sl]
            dg = one if dg is None else dg + one
        dgm = jnp.concatenate([jnp.where(chunk == c, dg, 0.0).astype(BF16) for c in range(chunks)], axis=0)
        dtab[...] += mm_nt(one_src[:, sl], dgm)
        return carry

    lax.fori_loop(0, edges // block, scatter, 0)

    for c in range(chunks):
        dtab_out[c * CHUNK : (c + 1) * CHUNK, :] = dtab[:, c * width : (c + 1) * width].astype(BF16)
    returns = [
        to_peer(
            p,
            dtab_out.at[pl.ds(owned + p * slots, slots)],
            back.at[pl.ds(p * slots, slots)],
            back_send,
            back_recv,
            -1,
        )
        for p in range(6)
    ]
    for copy in returns:
        copy.start()

    if comm:

        @pl.when(owner)
        def _():
            all_one.wait_recv()
            total = ar_half[rows_of(my_slice), :].astype(F32)
            for s in range(1, group):
                total = total + got_one[s].astype(F32)
            got_two[plane] = total.astype(BF16)
            loop(1, planes, lambda s: copy_two(s).start())

    def sums(b, carry):
        sl = pl.ds(pl.multiple_of(b * 256, 256), 256)
        for deg in range(3):
            w = radial[deg * width : (deg + 1) * width, sl] * gathered[:, sl]
            for m in range(1, 9):
                if DEGREE[m] == deg:
                    d = dterms[m * width : (m + 1) * width, sl].astype(F32)
                    dharm[m - 1 : m, sl] = jnp.sum(w * d, axis=0, keepdims=True)
        return carry

    lax.fori_loop(0, edges // 256, sums, 0, unroll=2)

    if comm:

        @pl.when(owner)
        def _():
            all_two.wait_recv()
            total = got_two[0].astype(F32)
            for s in range(1, planes):
                total = total + got_two[s].astype(F32)
            half_three[...] = total.astype(BF16)
            plane_loop(lambda u: copy_three(u).start(), FAR_FIRST)
            own = pltpu.make_async_copy(half_three, final.at[rows_of(my_slice)], own_sem)
            own.start()
            own.wait()

    dbas = mm(w1_both, dpre[...])
    ddist = jnp.sum((dbas[:8] + dbas[8:]) * dbasis[...], axis=0, keepdims=True)
    ux, uy, uz, inv = (geom[i : i + 1, :] for i in range(4))
    g1, g2, g3, g4, g5, g6, g7, g8 = (dharm[i : i + 1, :] for i in range(8))
    dx = r3 * g1 + r15 * (g4 * uy + g7 * uz + g8 * ux)
    dy = r3 * g2 + r15 * (g4 * ux + g5 * uz - g8 * uy)
    dz = r3 * g3 + r15 * (g5 * uy + g7 * ux) + (3.0 * r5) * (uz * g6)
    dd = ddist - (dx * ux + dy * uy + dz * uz) * inv
    force[0:1, :] = dx * inv + ux * dd
    force[1:2, :] = dy * inv + uy * dd
    force[2:3, :] = dz * inv + uz * dd

    for deg in range(3):
        hi, lo = mix_hl[deg]
        mix_t = jnp.concatenate([mm_nt(eye128, hi), mm_nt(eye128, lo)], axis=1).astype(BF16)
        for m in range(9):
            if DEGREE[m] == deg:
                out_t = mm(mix_t, jnp.concatenate([accb[m], accb[m]], axis=0)).astype(BF16)
                mixed[:, m * width : (m + 1) * width] = out_t.T
    stores = [
        pltpu.make_async_copy(a, b, out_sem.at[i])
        for i, (a, b) in enumerate(((mixed, mixed_far), (grad_feat, grad_feat_far), (force, force_far)))
    ]
    stores[0].start()
    stores[2].start()

    for copy in returns:
        if comm:
            copy.wait_recv()
        else:
            copy.wait()
    total = dtab[:, 0:width]
    for p in range(6):
        total = total + mm(picks(p), back[p * slots : (p + 1) * slots, :])
    grad_feat[...] = total
    stores[1].start()

    if comm:
        for copy in ghosts:
            copy.wait_send()
        for copy in returns:
            copy.wait_send()

        @pl.when(owner)
        def _():
            most_rows.wait_send()
            all_two.wait_send()
            loop(1, group, lambda s: copy_three(member).wait_send())
            most_rows.wait_recv()

        @pl.when(jnp.logical_not(owner))
        def _():
            all_rows.wait_send()
            all_rows.wait_recv()

    else:
        own = pltpu.make_async_copy(ar_half, final, own_sem)
        own.start()
        own.wait()
    for store in stores:
        store.wait()


def finish(*refs):
    inputs, outputs = refs[:4], refs[4:10]
    near, grads, in_sem, out_sem = refs[10:14], refs[14:17], refs[17], refs[18]
    loads = [pltpu.make_async_copy(a, b, in_sem.at[i]) for i, (a, b) in enumerate(zip(inputs, near))]
    stores = [
        pltpu.make_async_copy(a, b, out_sem.at[i])
        for i, (a, b) in enumerate(zip((*near[:3], *grads), outputs))
    ]
    for i in (3, 0, 1, 2):
        loads[i].start()
    rows = near[3]
    grad_one, grad_two, grad_mix = grads
    width = rows.shape[1]
    loads[3].wait()
    for deg in range(3):
        grad_mix[deg] = rows[deg * width : (deg + 1) * width, :].astype(F32)
    stores[5].start()
    row = 3 * width
    for deg in range(3):
        grad_two[:, deg * width : (deg + 1) * width] = rows[row : row + 64, :].astype(F32)
        row += 64
    stores[4].start()
    grad_one[...] = rows[row : row + 16, :].astype(F32)[0:8, 0:64]
    stores[3].start()
    for i in (0, 1, 2):
        loads[i].wait()
        stores[i].start()
    for store in stores:
        store.wait()


def on_device(
    nx,
    ny,
    block,
    features,
    edge_vec,
    edge_src,
    edge_dst,
    edge_count,
    send_gx,
    send_gy,
    w_one,
    w_two,
    mix,
    cotangent,
):
    owned, width = features.shape
    edges = edge_vec.shape[1]
    slots = send_gx.shape[1]
    hid = w_one.shape[1]
    rows = -(-(owned + 6 * slots) // CHUNK) * CHUNK
    chunks = rows // CHUNK
    group = PLANE_X * ny
    planes = max(nx // PLANE_X, 2)
    vmem = pl.BlockSpec(memory_space=pltpu.VMEM)
    far = pl.BlockSpec(memory_space=pl.ANY)
    dma = pltpu.SemaphoreType.DMA
    args = (
        features,
        edge_vec,
        edge_src.reshape(1, edges),
        edge_dst.reshape(1, edges),
        edge_count.reshape(1, 1),
        send_gx,
        send_gy,
        w_one,
        w_two,
        mix,
        cotangent,
    )
    shapes = (
        jax.ShapeDtypeStruct((owned, 9 * width), BF16),
        jax.ShapeDtypeStruct((owned, width), F32),
        jax.ShapeDtypeStruct((3, edges), F32),
    )
    scratch = [
        *(pltpu.VMEM(a.shape, a.dtype) for a in args),
        *(pltpu.VMEM(a.shape, a.dtype) for a in shapes),
        pltpu.VMEM((rows, width), BF16),
        pltpu.VMEM((6 * slots, width), BF16),
        pltpu.VMEM((rows, width), BF16),
        pltpu.VMEM((6 * slots, width), BF16),
        pltpu.VMEM((CHUNK, chunks * width), F32),
        pltpu.VMEM((9 * width, owned), F32),
        pltpu.VMEM((9 * width, owned), BF16),
        pltpu.VMEM((CHUNK, edges), BF16),
        pltpu.VMEM((owned, edges), BF16),
        pltpu.VMEM((3 * width, edges), F32),
        pltpu.VMEM((3 * width, edges), F32),
        pltpu.VMEM((9 * width, edges), BF16),
        pltpu.VMEM((hid, edges), F32),
        pltpu.VMEM((hid, edges), BF16),
        pltpu.VMEM((8, edges), F32),
        pltpu.VMEM((16, edges), BF16),
        pltpu.VMEM((8, edges), F32),
        pltpu.VMEM((8, edges), F32),
        pltpu.VMEM((1, edges), jnp.int32),
        pltpu.VMEM((8, edges), F32),
        pltpu.VMEM((hid, 3 * width), F32),
        pltpu.VMEM((hid, edges), BF16),
        pltpu.VMEM((width, edges), F32),
        pltpu.VMEM((SLICES * SLICE, width), BF16),
        pltpu.VMEM((group, SLICE, width), BF16),
        pltpu.VMEM((planes, SLICE, width), BF16),
        pltpu.VMEM((SLICE, width), BF16),
        dma((6,)),
        dma((6,)),
        dma((6,)),
        dma((6,)),
        dma,
        dma,
        dma,
        dma,
        dma,
        dma,
        dma,
        dma((11,)),
        dma((3,)),
    ]
    params = {"vmem_limit_bytes": 60 * 1024 * 1024}
    if nx > 1:
        params.update(collective_id=0, has_side_effects=True)
    mixed, grad_feat, force, final = pl.pallas_call(
        functools.partial(kernel, nx, ny, block),
        out_shape=(*shapes, jax.ShapeDtypeStruct((SLICES * SLICE, width), BF16)),
        in_specs=[far] * 11,
        out_specs=(far,) * 4,
        scratch_shapes=scratch,
        compiler_params=pltpu.CompilerParams(**params),
        name="interaction",
    )(*args)
    grads = tuple(jax.ShapeDtypeStruct(w.shape, F32) for w in (w_one, w_two, mix))
    return pl.pallas_call(
        finish,
        out_shape=(*shapes, *grads),
        in_specs=[far] * 4,
        out_specs=(far,) * 6,
        scratch_shapes=[
            *(pltpu.VMEM(a.shape, a.dtype) for a in (*shapes, final, *grads)),
            dma((4,)),
            dma((6,)),
        ],
        name="finish",
    )(mixed, grad_feat, force, final)


def solution(mesh, block=2048):
    tiles = ("gx", "gy")
    return jax.shard_map(
        functools.partial(on_device, mesh.shape["gx"], mesh.shape["gy"], block),
        mesh=mesh,
        in_specs=(
            P(tiles, None),
            P(None, tiles),
            P(tiles),
            P(tiles),
            P(tiles),
            P(tiles, None),
            P(tiles, None),
            P(),
            P(),
            P(),
            P(tiles, None),
        ),
        out_specs=(
            P(tiles, None),
            P(tiles, None),
            P(None, tiles),
            P(),
            P(),
            P(),
        ),
        check_vma=False,
    )
```

```python
import functools
import math

import jax
import jax.numpy as jnp
from jax import lax
from jax.experimental import pallas as pl
from jax.experimental.pallas import tpu as pltpu
from jax.sharding import PartitionSpec as P

F32 = jnp.float32
BF16 = jnp.bfloat16
DEGREE = [0, 1, 1, 1, 2, 2, 2, 2, 2]
ROW_STEPS = [1, -1, 2, -2]
COLUMN_STEPS = [1, -1]
CHUNK = 256
SLICE = 32
SLICES = 19
PLANE_X = 4
SPREAD = 5
SPREAD_INVERSE = 13
NEAR_FIRST = (0, 1, 3, 2)
FAR_FIRST = (2, 1, 3, 0)


def mm(a, b):
    return jnp.dot(a, b, preferred_element_type=F32)


def mm_nt(a, b):
    return lax.dot_general(a, b, (((1,), (1,)), ((), ())), preferred_element_type=F32)


def eye(n):
    rows = lax.broadcasted_iota(jnp.int32, (n, n), 0)
    cols = lax.broadcasted_iota(jnp.int32, (n, n), 1)
    return jnp.where(rows == cols, 1.0, 0.0).astype(BF16)


def split(a):
    hi = a.astype(BF16)
    lo = (a - hi.astype(F32)).astype(BF16)
    return hi, lo


def kernel(
    nx,
    ny,
    block,
    *refs,
):
    inputs = refs[:11]
    mixed_far, grad_feat_far, force_far, final = refs[11:15]
    near = refs[15:26]
    (
        features,
        vec,
        src,
        dst,
        count,
        send_x,
        send_y,
        w_one,
        w_two,
        mix,
        cot,
    ) = near
    (
        mixed,
        grad_feat,
        force,
        table,
        outgoing,
        dtab_out,
        back,
        dtab,
        acc,
        dacc,
        one_src,
        one_dst,
        radial,
        dweight,
        dterms,
        dsilu,
        hidden,
        harm,
        basis2,
        dbasis,
        geom,
        part,
        dharm,
        dw_two,
        dpre,
        gathered,
        ar_half,
        got_one,
        got_two,
        half_three,
        ghost_send,
        ghost_recv,
        back_send,
        back_recv,
        one_send,
        one_recv,
        two_send,
        two_recv,
        three_send,
        three_recv,
        own_sem,
        in_sem,
        out_sem,
    ) = refs[26:]
    owned, width = features.shape
    edges = vec.shape[1]
    slots = send_x.shape[1]
    comm = nx > 1
    chunks = table.shape[0] // CHUNK
    me_x = lax.axis_index("gx")
    me_y = lax.axis_index("gy")
    factor = math.sqrt(owned / edges)
    group = PLANE_X * ny
    planes = nx // PLANE_X
    plane = lax.div(me_x, PLANE_X)
    member = lax.rem(me_x, PLANE_X) * ny + me_y
    my_slice = lax.rem(member * SPREAD_INVERSE, group)
    owner = my_slice < SLICES

    def loop(low, high, f):
        def step(s, c):
            f(s)
            return c

        lax.fori_loop(low, high, step, 0)

    def plane_loop(f, order):
        for step in order:
            column = lax.rem(lax.rem(me_x, PLANE_X) + step, PLANE_X) * ny
            loop(1 if step == 0 else 0, ny, lambda s: f(column + lax.rem(me_y + s, ny)))

    def in_plane(u):
        return {"gx": plane * PLANE_X + lax.div(u, ny), "gy": lax.rem(u, ny)}

    def along(s):
        return {"gx": lax.rem(me_x + s + nx, nx)}

    def across(s):
        return {"gy": lax.rem(me_y + s + ny, ny)}

    if comm:
        barrier = pltpu.get_barrier_semaphore()

        def greet(where):
            pl.semaphore_signal(barrier, inc=1, device_id=where, device_id_type=pl.DeviceIdType.MESH)

        for s in ROW_STEPS:
            greet(along(s))
        loop(1, planes, lambda s: greet(along(s * PLANE_X)))
        plane_loop(lambda u: greet(in_plane(u)), NEAR_FIRST)

    loads = [pltpu.make_async_copy(a, b, in_sem.at[i]) for i, (a, b) in enumerate(zip(inputs, near))]
    for i in (0, 5, 6, 10, 9, 8, 7, 1, 2, 3, 4):
        loads[i].start()

    def remote(where, source, target, send, recv):
        return pltpu.make_async_remote_copy(
            src_ref=source,
            dst_ref=target,
            send_sem=send,
            recv_sem=recv,
            device_id=where,
            device_id_type=pl.DeviceIdType.MESH,
        )

    def to_peer(p, source, target, sends, recvs, sign):
        where = along(sign * ROW_STEPS[p]) if p < 4 else across(sign * COLUMN_STEPS[p - 4])
        if not comm:
            return pltpu.make_async_copy(source, target, recvs.at[p])
        return remote(where, source, target, sends.at[p], recvs.at[p])

    eye128 = eye(128)
    for i in (0, 5, 6):
        loads[i].wait()
    feats = features[...]

    def picks(p):
        row = send_x[p : p + 1, :] if p < 4 else send_y[p - 4 : p - 3, :]
        rows = lax.broadcasted_iota(jnp.int32, (owned, slots), 0)
        return jnp.where(rows == row, 1.0, 0.0).astype(BF16)

    for p in range(6):
        outgoing[p * slots : (p + 1) * slots, :] = mm(picks(p).T, feats).astype(BF16)
    if comm:
        pl.semaphore_wait(barrier, group + planes + len(ROW_STEPS) - 2)
    ghosts = [
        to_peer(
            p,
            outgoing.at[pl.ds(p * slots, slots)],
            table.at[pl.ds(owned + p * slots, slots)],
            ghost_send,
            ghost_recv,
            1,
        )
        for p in range(6)
    ]
    for copy in ghosts:
        copy.start()

    dtab[...] = jnp.zeros_like(dtab)
    acc[...] = jnp.zeros_like(acc)
    dw_two[...] = jnp.zeros_like(dw_two)
    table[0:owned, :] = feats
    used = owned + 6 * slots
    table[used:, :] = jnp.zeros((table.shape[0] - used, width), BF16)

    for i in (7, 8, 9, 1, 2, 3, 4):
        loads[i].wait()
    w1h, w1l = split(w_one[...])
    w1h = w1h.astype(F32)
    w1l = w1l.astype(F32)
    w1_both = jnp.concatenate([w1h, w1l], axis=0).astype(BF16)
    w1_stack = jnp.concatenate([w1h, w1h, w1l, jnp.zeros_like(w1l)], axis=0).astype(BF16)
    w1_t = mm_nt(eye128[:64, :64], w1_stack).astype(BF16)
    w2h, w2l = split(w_two[...])
    w2_both = jnp.concatenate([w2h, w2l], axis=0)
    w2_stack = jnp.concatenate([w2h, w2h, w2l], axis=0)
    w2_t = jnp.concatenate(
        [w2_stack[:, deg * width : (deg + 1) * width].T for deg in range(3)],
        axis=0,
    )
    mix_hl = [split(mix[deg]) for deg in range(3)]
    loads[10].wait()
    for m in range(9):
        hi, lo = mix_hl[DEGREE[m]]
        cot_m = cot[:, m * width : (m + 1) * width]
        both = mm_nt(jnp.concatenate([hi, lo], axis=1), jnp.concatenate([cot_m, cot_m], axis=1))
        dacc[m * width : (m + 1) * width, :] = (both * factor).astype(BF16)

    live_count = count[...]
    r3 = math.sqrt(3.0)
    r5 = math.sqrt(5.0)
    r15 = math.sqrt(15.0)
    pi = math.pi

    def part_one(block):
        sl = pl.ds(0, block)
        index = src[:, sl]
        chunk = lax.shift_right_logical(index, 8)
        part[:, sl] = chunk
        rows = lax.broadcasted_iota(jnp.int32, (CHUNK, block), 0)
        one_src[:, sl] = jnp.where(rows == index - chunk * CHUNK, 1.0, 0.0).astype(BF16)
        one_dst[:, sl] = jnp.where(rows == dst[:, sl], 1.0, 0.0).astype(BF16)
        dall = mm(dacc[...], one_dst[:, sl])
        dterms[:, sl] = dall.astype(BF16)

        v = vec[:, sl]
        x, y, z = v[0:1], v[1:2], v[2:3]
        dist = jnp.sqrt(x * x + y * y + z * z + 0.25)
        inv = 1.0 / dist
        ratio = dist * (1.0 / 5.0)
        ra2 = ratio * ratio
        ra5 = ra2 * ra2 * ratio
        env = 1.0 / (1.0 + ra5 * ratio)
        ux, uy, uz = x * inv, y * inv, z * inv
        geom[0:1, sl] = ux
        geom[1:2, sl] = uy
        geom[2:3, sl] = uz
        geom[3:4, sl] = inv
        hs = [
            r3 * ux,
            r3 * uy,
            r3 * uz,
            r15 * ux * uy,
            r15 * uy * uz,
            0.5 * r5 * (3.0 * uz * uz - 1.0),
            r15 * ux * uz,
            0.5 * r15 * (ux * ux - uy * uy),
        ]
        for i in range(8):
            harm[i : i + 1, sl] = hs[i]
        k = (lax.broadcasted_iota(jnp.int32, (8, block), 0) + 1).astype(F32)
        t = k * ratio
        n = jnp.floor(t + 0.5)
        r = t - n
        sgn = 1.0 - 2.0 * (n - 2.0 * jnp.floor(n * 0.5))
        q = r * r
        s_pi = pi**9 / 362880.0 - q * (pi**11 / 39916800.0)
        s_pi = pi**7 / 5040.0 - q * s_pi
        s_pi = pi**5 / 120.0 - q * s_pi
        s_pi = pi**3 / 6.0 - q * s_pi
        s_pi = r * (pi - q * s_pi)
        c_pi = pi**10 / 3628800.0 - q * (pi**12 / 479001600.0)
        c_pi = pi**8 / 40320.0 - q * c_pi
        c_pi = pi**6 / 720.0 - q * c_pi
        c_pi = pi**4 / 24.0 - q * c_pi
        c_pi = pi**2 / 2.0 - q * c_pi
        c_pi = 1.0 - q * c_pi
        amp = sgn * (inv * env)
        bas = s_pi * amp
        dbasis[:, sl] = c_pi * amp * (k * (pi / 5.0)) - bas * (inv + (6.0 / 5.0) * (env * ra5))
        bh = bas.astype(BF16).astype(F32)
        bl = bas - bh
        basis2[:, sl] = jnp.concatenate([bh, bl], axis=0).astype(BF16)
        bstack = jnp.concatenate([bh, bl, bh, jnp.zeros_like(bh)], axis=0).astype(BF16)
        pre = mm(w1_t, bstack)
        spot = lax.broadcasted_iota(jnp.int32, (1, block), 1)
        live = jnp.where(spot < live_count, 1.0, 0.0)
        sig = 1.0 / (1.0 + jnp.exp(-pre))
        sig_live = sig * live
        hid = pre * sig_live
        dsilu[:, sl] = sig_live * (1.0 + pre * (1.0 - sig))
        hh, hl = split(hid)
        hidden[:, sl] = hh
        radial[:, sl] = mm(w2_t, jnp.concatenate([hh, hl, hh], axis=0))

        for deg, ms in enumerate(((0,), (1, 2, 3), (4, 5, 6, 7, 8))):
            total = None
            for m in ms:
                term = dall[m * width : (m + 1) * width]
                if m > 0:
                    term = term * hs[m - 1]
                total = term if total is None else total + term
            dweight[deg * width : (deg + 1) * width, sl] = total

    part_one(edges)

    for copy in ghosts:
        if comm:
            copy.wait_recv()
        else:
            copy.wait()
    table_t = jnp.concatenate(
        [table[c * CHUNK : (c + 1) * CHUNK, :].T for c in range(chunks)], axis=0
    )

    def gather(b):
        sl = pl.ds(pl.multiple_of(b * block, block), block)
        chunk = part[:, sl]
        got = mm(table_t, one_src[:, sl])
        g = got[0:width]
        for c in range(1, chunks):
            g = jnp.where(chunk == c, got[c * width : (c + 1) * width], g)
        gathered[:, sl] = g

    def part_two(b, carry):
        sl = pl.ds(pl.multiple_of(b * block, block), block)
        gather(b)
        g = gathered[:, sl]
        drad = jnp.concatenate(
            [(dweight[deg * width : (deg + 1) * width, sl] * g).astype(BF16) for deg in range(3)], axis=0
        )
        weighted = [radial[deg * width : (deg + 1) * width, sl] * g for deg in range(3)]
        halves = [w.astype(BF16) for w in weighted]
        terms = [halves[0]]
        for m in range(1, 9):
            terms.append(halves[DEGREE[m]] * harm[m - 1 : m, sl].astype(BF16))
        dhid = mm(w2_both, drad)
        dw_two[...] += mm_nt(hidden[:, sl], drad)
        acc[...] += (mm_nt(jnp.concatenate(terms, axis=0), one_dst[:, sl]))
        dpre[:, sl] = ((dhid[:64] + dhid[64:]) * dsilu[:, sl]).astype(BF16)
        return carry

    lax.fori_loop(0, edges // block, part_two, 0)
    dw_one = mm_nt(basis2[...], dpre[...])

    accb = [(acc[m * width : (m + 1) * width, :] * factor).astype(BF16) for m in range(9)]
    for deg in range(3):
        total = None
        for m in range(9):
            if DEGREE[m] == deg:
                one = mm(accb[m], cot[:, m * width : (m + 1) * width])
                total = one if total is None else total + one
        ar_half[deg * width : (deg + 1) * width, :] = total.astype(BF16)
    row = 3 * width
    for deg in range(3):
        ar_half[row : row + 64, :] = dw_two[:, deg * width : (deg + 1) * width].astype(BF16)
        row += 64
    tail = jnp.concatenate([dw_one[0:8, :] + dw_one[8:16, :], jnp.zeros((8, 64), F32)], axis=0)
    tail = jnp.concatenate([tail, jnp.zeros((16, 64), F32)], axis=1)
    ar_half[row : row + 16, :] = tail.astype(BF16)
    ar_half[row + 16 :, :] = jnp.zeros((ar_half.shape[0] - row - 16, width), BF16)

    def rows_of(q):
        return pl.ds(pl.multiple_of(q * SLICE, SLICE), SLICE)

    def copy_one(u, q):
        slot = lax.rem(member - u + group, group)
        return remote(in_plane(u), ar_half.at[rows_of(q)], got_one.at[slot], one_send, one_recv)

    def copy_two(s):
        return remote(along(s * PLANE_X), got_two.at[plane], got_two.at[plane], two_send, two_recv)

    def copy_three(u):
        return remote(in_plane(u), half_three, final.at[rows_of(my_slice)], three_send, three_recv)

    here = {"gx": me_x, "gy": me_y}
    all_one = remote(here, got_one.at[pl.ds(1, group - 1)], got_one.at[pl.ds(1, group - 1)], one_send, one_recv)
    all_two = remote(here, got_two.at[pl.ds(1, planes - 1)], got_two.at[pl.ds(1, planes - 1)], two_send, two_recv)
    most = pl.ds(0, (SLICES - 1) * SLICE)
    all_rows = remote(here, ar_half, final, one_send, three_recv)
    most_rows = remote(here, ar_half.at[most], final.at[most], one_send, three_recv)

    if comm:

        def send_one(u):
            q = lax.rem(u * SPREAD_INVERSE, group)

            @pl.when(q < SLICES)
            def _():
                copy_one(u, q).start()

        plane_loop(send_one, FAR_FIRST)

    def scatter(b, carry):
        sl = pl.ds(pl.multiple_of(b * block, block), block)
        chunk = part[:, sl]
        dg = None
        for deg in range(3):
            rws = slice(deg * width, (deg + 1) * width)
            one = radial[rws, sl] * dweight[rws, sl]
            dg = one if dg is None else dg + one
        dgm = jnp.concatenate([jnp.where(chunk == c, dg, 0.0).astype(BF16) for c in range(chunks)], axis=0)
        dtab[...] += mm_nt(one_src[:, sl], dgm)
        return carry

    lax.fori_loop(0, edges // block, scatter, 0)

    for c in range(chunks):
        dtab_out[c * CHUNK : (c + 1) * CHUNK, :] = dtab[:, c * width : (c + 1) * width].astype(BF16)
    returns = [
        to_peer(
            p,
            dtab_out.at[pl.ds(owned + p * slots, slots)],
            back.at[pl.ds(p * slots, slots)],
            back_send,
            back_recv,
            -1,
        )
        for p in range(6)
    ]
    for copy in returns:
        copy.start()

    if comm:

        @pl.when(owner)
        def _():
            all_one.wait_recv()
            total = ar_half[rows_of(my_slice), :].astype(F32)
            for s in range(1, group):
                total = total + got_one[s].astype(F32)
            got_two[plane] = total.astype(BF16)
            loop(1, planes, lambda s: copy_two(s).start())

    def sums(b, carry):
        sl = pl.ds(pl.multiple_of(b * 256, 256), 256)
        for deg in range(3):
            w = radial[deg * width : (deg + 1) * width, sl] * gathered[:, sl]
            for m in range(1, 9):
                if DEGREE[m] == deg:
                    d = dterms[m * width : (m + 1) * width, sl].astype(F32)
                    dharm[m - 1 : m, sl] = jnp.sum(w * d, axis=0, keepdims=True)
        return carry

    lax.fori_loop(0, edges // 256, sums, 0, unroll=2)

    if comm:

        @pl.when(owner)
        def _():
            all_two.wait_recv()
            total = got_two[0].astype(F32)
            for s in range(1, planes):
                total = total + got_two[s].astype(F32)
            half_three[...] = total.astype(BF16)
            plane_loop(lambda u: copy_three(u).start(), FAR_FIRST)
            own = pltpu.make_async_copy(half_three, final.at[rows_of(my_slice)], own_sem)
            own.start()
            own.wait()

    dbas = mm(w1_both, dpre[...])
    ddist = jnp.sum((dbas[:8] + dbas[8:]) * dbasis[...], axis=0, keepdims=True)
    ux, uy, uz, inv = (geom[i : i + 1, :] for i in range(4))
    g1, g2, g3, g4, g5, g6, g7, g8 = (dharm[i : i + 1, :] for i in range(8))
    dx = r3 * g1 + r15 * (g4 * uy + g7 * uz + g8 * ux)
    dy = r3 * g2 + r15 * (g4 * ux + g5 * uz - g8 * uy)
    dz = r3 * g3 + r15 * (g5 * uy + g7 * ux) + (3.0 * r5) * (uz * g6)
    dd = ddist - (dx * ux + dy * uy + dz * uz) * inv
    force[0:1, :] = dx * inv + ux * dd
    force[1:2, :] = dy * inv + uy * dd
    force[2:3, :] = dz * inv + uz * dd

    for deg in range(3):
        hi, lo = mix_hl[deg]
        mix_t = jnp.concatenate([mm_nt(eye128, hi), mm_nt(eye128, lo)], axis=1).astype(BF16)
        for m in range(9):
            if DEGREE[m] == deg:
                out_t = mm(mix_t, jnp.concatenate([accb[m], accb[m]], axis=0)).astype(BF16)
                mixed[:, m * width : (m + 1) * width] = out_t.T
    stores = [
        pltpu.make_async_copy(a, b, out_sem.at[i])
        for i, (a, b) in enumerate(((mixed, mixed_far), (grad_feat, grad_feat_far), (force, force_far)))
    ]
    stores[0].start()
    stores[2].start()

    for copy in returns:
        if comm:
            copy.wait_recv()
        else:
            copy.wait()
    total = dtab[:, 0:width]
    for p in range(6):
        total = total + mm(picks(p), back[p * slots : (p + 1) * slots, :])
    grad_feat[...] = total
    stores[1].start()

    if comm:
        for copy in ghosts:
            copy.wait_send()
        for copy in returns:
            copy.wait_send()

        @pl.when(owner)
        def _():
            most_rows.wait_send()
            all_two.wait_send()
            loop(1, group, lambda s: copy_three(member).wait_send())
            most_rows.wait_recv()

        @pl.when(jnp.logical_not(owner))
        def _():
            all_rows.wait_send()
            all_rows.wait_recv()

    else:
        own = pltpu.make_async_copy(ar_half, final, own_sem)
        own.start()
        own.wait()
    for store in stores:
        store.wait()


def finish(*refs):
    inputs, outputs = refs[:4], refs[4:10]
    near, grads, in_sem, out_sem = refs[10:14], refs[14:17], refs[17], refs[18]
    loads = [pltpu.make_async_copy(a, b, in_sem.at[i]) for i, (a, b) in enumerate(zip(inputs, near))]
    stores = [
        pltpu.make_async_copy(a, b, out_sem.at[i])
        for i, (a, b) in enumerate(zip((*near[:3], *grads), outputs))
    ]
    for i in (3, 0, 1, 2):
        loads[i].start()
    rows = near[3]
    grad_one, grad_two, grad_mix = grads
    width = rows.shape[1]
    loads[3].wait()
    for deg in range(3):
        grad_mix[deg] = rows[deg * width : (deg + 1) * width, :].astype(F32)
    stores[5].start()
    row = 3 * width
    for deg in range(3):
        grad_two[:, deg * width : (deg + 1) * width] = rows[row : row + 64, :].astype(F32)
        row += 64
    stores[4].start()
    grad_one[...] = rows[row : row + 16, :].astype(F32)[0:8, 0:64]
    stores[3].start()
    for i in (0, 1, 2):
        loads[i].wait()
        stores[i].start()
    for store in stores:
        store.wait()


def on_device(
    nx,
    ny,
    block,
    features,
    edge_vec,
    edge_src,
    edge_dst,
    edge_count,
    send_gx,
    send_gy,
    w_one,
    w_two,
    mix,
    cotangent,
):
    owned, width = features.shape
    edges = edge_vec.shape[1]
    slots = send_gx.shape[1]
    hid = w_one.shape[1]
    rows = -(-(owned + 6 * slots) // CHUNK) * CHUNK
    chunks = rows // CHUNK
    group = PLANE_X * ny
    planes = max(nx // PLANE_X, 2)
    vmem = pl.BlockSpec(memory_space=pltpu.VMEM)
    far = pl.BlockSpec(memory_space=pl.ANY)
    dma = pltpu.SemaphoreType.DMA
    args = (
        features,
        edge_vec,
        edge_src.reshape(1, edges),
        edge_dst.reshape(1, edges),
        edge_count.reshape(1, 1),
        send_gx,
        send_gy,
        w_one,
        w_two,
        mix,
        cotangent,
    )
    shapes = (
        jax.ShapeDtypeStruct((owned, 9 * width), BF16),
        jax.ShapeDtypeStruct((owned, width), F32),
        jax.ShapeDtypeStruct((3, edges), F32),
    )
    scratch = [
        *(pltpu.VMEM(a.shape, a.dtype) for a in args),
        *(pltpu.VMEM(a.shape, a.dtype) for a in shapes),
        pltpu.VMEM((rows, width), BF16),
        pltpu.VMEM((6 * slots, width), BF16),
        pltpu.VMEM((rows, width), BF16),
        pltpu.VMEM((6 * slots, width), BF16),
        pltpu.VMEM((CHUNK, chunks * width), F32),
        pltpu.VMEM((9 * width, owned), F32),
        pltpu.VMEM((9 * width, owned), BF16),
        pltpu.VMEM((CHUNK, edges), BF16),
        pltpu.VMEM((owned, edges), BF16),
        pltpu.VMEM((3 * width, edges), F32),
        pltpu.VMEM((3 * width, edges), F32),
        pltpu.VMEM((9 * width, edges), BF16),
        pltpu.VMEM((hid, edges), F32),
        pltpu.VMEM((hid, edges), BF16),
        pltpu.VMEM((8, edges), F32),
        pltpu.VMEM((16, edges), BF16),
        pltpu.VMEM((8, edges), F32),
        pltpu.VMEM((8, edges), F32),
        pltpu.VMEM((1, edges), jnp.int32),
        pltpu.VMEM((8, edges), F32),
        pltpu.VMEM((hid, 3 * width), F32),
        pltpu.VMEM((hid, edges), BF16),
        pltpu.VMEM((width, edges), F32),
        pltpu.VMEM((SLICES * SLICE, width), BF16),
        pltpu.VMEM((group, SLICE, width), BF16),
        pltpu.VMEM((planes, SLICE, width), BF16),
        pltpu.VMEM((SLICE, width), BF16),
        dma((6,)),
        dma((6,)),
        dma((6,)),
        dma((6,)),
        dma,
        dma,
        dma,
        dma,
        dma,
        dma,
        dma,
        dma((11,)),
        dma((3,)),
    ]
    params = {"vmem_limit_bytes": 60 * 1024 * 1024}
    if nx > 1:
        params.update(collective_id=0, has_side_effects=True)
    mixed, grad_feat, force, final = pl.pallas_call(
        functools.partial(kernel, nx, ny, block),
        out_shape=(*shapes, jax.ShapeDtypeStruct((SLICES * SLICE, width), BF16)),
        in_specs=[far] * 11,
        out_specs=(far,) * 4,
        scratch_shapes=scratch,
        compiler_params=pltpu.CompilerParams(**params),
        name="interaction",
    )(*args)
    grads = tuple(jax.ShapeDtypeStruct(w.shape, F32) for w in (w_one, w_two, mix))
    return pl.pallas_call(
        finish,
        out_shape=(*shapes, *grads),
        in_specs=[far] * 4,
        out_specs=(far,) * 6,
        scratch_shapes=[
            *(pltpu.VMEM(a.shape, a.dtype) for a in (*shapes, final, *grads)),
            dma((4,)),
            dma((6,)),
        ],
        name="finish",
    )(mixed, grad_feat, force, final)


def solution(mesh, block=2048):
    tiles = ("gx", "gy")
    return jax.shard_map(
        functools.partial(on_device, mesh.shape["gx"], mesh.shape["gy"], block),
        mesh=mesh,
        in_specs=(
            P(tiles, None),
            P(None, tiles),
            P(tiles),
            P(tiles),
            P(tiles),
            P(tiles, None),
            P(tiles, None),
            P(),
            P(),
            P(),
            P(tiles, None),
        ),
        out_specs=(
            P(tiles, None),
            P(tiles, None),
            P(None, tiles),
            P(),
            P(),
            P(),
        ),
        check_vma=False,
    )
```

```python
import functools
import math

import jax
import jax.numpy as jnp
from jax import lax
from jax.experimental import pallas as pl
from jax.experimental.pallas import tpu as pltpu
from jax.sharding import PartitionSpec as P

F32 = jnp.float32
BF16 = jnp.bfloat16
DEGREE = [0, 1, 1, 1, 2, 2, 2, 2, 2]
ROW_STEPS = [1, -1, 2, -2]
COLUMN_STEPS = [1, -1]
CHUNK = 256
SLICE = 32
SLICES = 19
PLANE_X = 4
SPREAD = 5
SPREAD_INVERSE = 13
NEAR_FIRST = (0, 1, 3, 2)
FAR_FIRST = (2, 1, 3, 0)


def mm(a, b):
    return jnp.dot(a, b, preferred_element_type=F32)


def mm_nt(a, b):
    return lax.dot_general(a, b, (((1,), (1,)), ((), ())), preferred_element_type=F32)


def eye(n):
    rows = lax.broadcasted_iota(jnp.int32, (n, n), 0)
    cols = lax.broadcasted_iota(jnp.int32, (n, n), 1)
    return jnp.where(rows == cols, 1.0, 0.0).astype(BF16)


def split(a):
    hi = a.astype(BF16)
    lo = (a - hi.astype(F32)).astype(BF16)
    return hi, lo


def kernel(
    nx,
    ny,
    block,
    *refs,
):
    inputs = refs[:11]
    mixed_far, grad_feat_far, force_far, final = refs[11:15]
    near = refs[15:26]
    (
        features,
        vec,
        src,
        dst,
        count,
        send_x,
        send_y,
        w_one,
        w_two,
        mix,
        cot,
    ) = near
    (
        mixed,
        grad_feat,
        force,
        table,
        outgoing,
        dtab_out,
        back,
        dtab,
        acc,
        dacc,
        one_src,
        one_dst,
        radial,
        dweight,
        dterms,
        dsilu,
        hidden,
        harm,
        basis2,
        dbasis,
        geom,
        part,
        dharm,
        dw_two,
        dpre,
        gathered,
        ar_half,
        got_one,
        got_two,
        half_three,
        ghost_send,
        ghost_recv,
        back_send,
        back_recv,
        one_send,
        one_recv,
        two_send,
        two_recv,
        three_send,
        three_recv,
        own_sem,
        in_sem,
        out_sem,
    ) = refs[26:]
    owned, width = features.shape
    edges = vec.shape[1]
    slots = send_x.shape[1]
    comm = nx > 1
    chunks = table.shape[0] // CHUNK
    me_x = lax.axis_index("gx")
    me_y = lax.axis_index("gy")
    factor = math.sqrt(owned / edges)
    group = PLANE_X * ny
    planes = nx // PLANE_X
    plane = lax.div(me_x, PLANE_X)
    member = lax.rem(me_x, PLANE_X) * ny + me_y
    my_slice = lax.rem(member * SPREAD_INVERSE, group)
    owner = my_slice < SLICES

    def loop(low, high, f):
        def step(s, c):
            f(s)
            return c

        lax.fori_loop(low, high, step, 0)

    def plane_loop(f, order):
        for step in order:
            column = lax.rem(lax.rem(me_x, PLANE_X) + step, PLANE_X) * ny
            loop(1 if step == 0 else 0, ny, lambda s: f(column + lax.rem(me_y + s, ny)))

    def in_plane(u):
        return {"gx": plane * PLANE_X + lax.div(u, ny), "gy": lax.rem(u, ny)}

    def along(s):
        return {"gx": lax.rem(me_x + s + nx, nx)}

    def across(s):
        return {"gy": lax.rem(me_y + s + ny, ny)}

    loads = [pltpu.make_async_copy(a, b, in_sem.at[i]) for i, (a, b) in enumerate(zip(inputs, near))]
    for i in (0, 5, 6, 10, 9, 8, 7, 1, 2, 3, 4):
        loads[i].start()

    if comm:
        barrier = pltpu.get_barrier_semaphore()

        def greet(where):
            pl.semaphore_signal(barrier, inc=1, device_id=where, device_id_type=pl.DeviceIdType.MESH)

        for s in ROW_STEPS:
            greet(along(s))
        loop(1, planes, lambda s: greet(along(s * PLANE_X)))
        plane_loop(lambda u: greet(in_plane(u)), NEAR_FIRST)

    def remote(where, source, target, send, recv):
        return pltpu.make_async_remote_copy(
            src_ref=source,
            dst_ref=target,
            send_sem=send,
            recv_sem=recv,
            device_id=where,
            device_id_type=pl.DeviceIdType.MESH,
        )

    def to_peer(p, source, target, sends, recvs, sign):
        where = along(sign * ROW_STEPS[p]) if p < 4 else across(sign * COLUMN_STEPS[p - 4])
        if not comm:
            return pltpu.make_async_copy(source, target, recvs.at[p])
        return remote(where, source, target, sends.at[p], recvs.at[p])

    eye128 = eye(128)
    for i in (0, 5, 6):
        loads[i].wait()
    feats = features[...]

    def picks(p):
        row = send_x[p : p + 1, :] if p < 4 else send_y[p - 4 : p - 3, :]
        rows = lax.broadcasted_iota(jnp.int32, (owned, slots), 0)
        return jnp.where(rows == row, 1.0, 0.0).astype(BF16)

    for p in range(6):
        outgoing[p * slots : (p + 1) * slots, :] = mm(picks(p).T, feats).astype(BF16)
    if comm:
        pl.semaphore_wait(barrier, group + planes + len(ROW_STEPS) - 2)
    ghosts = [
        to_peer(
            p,
            outgoing.at[pl.ds(p * slots, slots)],
            table.at[pl.ds(owned + p * slots, slots)],
            ghost_send,
            ghost_recv,
            1,
        )
        for p in range(6)
    ]
    for copy in ghosts:
        copy.start()

    dtab[...] = jnp.zeros_like(dtab)
    acc[...] = jnp.zeros_like(acc)
    dw_two[...] = jnp.zeros_like(dw_two)
    table[0:owned, :] = feats
    used = owned + 6 * slots
    table[used:, :] = jnp.zeros((table.shape[0] - used, width), BF16)

    for i in (7, 8, 9, 1, 2, 3, 4):
        loads[i].wait()
    w1h, w1l = split(w_one[...])
    w1h = w1h.astype(F32)
    w1l = w1l.astype(F32)
    w1_both = jnp.concatenate([w1h, w1l], axis=0).astype(BF16)
    w1_stack = jnp.concatenate([w1h, w1h, w1l, jnp.zeros_like(w1l)], axis=0).astype(BF16)
    w1_t = mm_nt(eye128[:64, :64], w1_stack).astype(BF16)
    w2h, w2l = split(w_two[...])
    w2_both = jnp.concatenate([w2h, w2l], axis=0)
    w2_stack = jnp.concatenate([w2h, w2h, w2l], axis=0)
    w2_t = jnp.concatenate(
        [w2_stack[:, deg * width : (deg + 1) * width].T for deg in range(3)],
        axis=0,
    )
    mix_hl = [split(mix[deg]) for deg in range(3)]
    loads[10].wait()
    for m in range(9):
        hi, lo = mix_hl[DEGREE[m]]
        cot_m = cot[:, m * width : (m + 1) * width]
        both = mm_nt(jnp.concatenate([hi, lo], axis=1), jnp.concatenate([cot_m, cot_m], axis=1))
        dacc[m * width : (m + 1) * width, :] = (both * factor).astype(BF16)

    live_count = count[...]
    r3 = math.sqrt(3.0)
    r5 = math.sqrt(5.0)
    r15 = math.sqrt(15.0)
    pi = math.pi

    def part_one(block):
        sl = pl.ds(0, block)
        index = src[:, sl]
        chunk = lax.shift_right_logical(index, 8)
        part[:, sl] = chunk
        rows = lax.broadcasted_iota(jnp.int32, (CHUNK, block), 0)
        one_src[:, sl] = jnp.where(rows == index - chunk * CHUNK, 1.0, 0.0).astype(BF16)
        one_dst[:, sl] = jnp.where(rows == dst[:, sl], 1.0, 0.0).astype(BF16)
        dall = mm(dacc[...], one_dst[:, sl])
        dterms[:, sl] = dall.astype(BF16)

        v = vec[:, sl]
        x, y, z = v[0:1], v[1:2], v[2:3]
        dist = jnp.sqrt(x * x + y * y + z * z + 0.25)
        inv = 1.0 / dist
        ratio = dist * (1.0 / 5.0)
        ra2 = ratio * ratio
        ra5 = ra2 * ra2 * ratio
        env = 1.0 / (1.0 + ra5 * ratio)
        ux, uy, uz = x * inv, y * inv, z * inv
        geom[0:1, sl] = ux
        geom[1:2, sl] = uy
        geom[2:3, sl] = uz
        geom[3:4, sl] = inv
        hs = [
            r3 * ux,
            r3 * uy,
            r3 * uz,
            r15 * ux * uy,
            r15 * uy * uz,
            0.5 * r5 * (3.0 * uz * uz - 1.0),
            r15 * ux * uz,
            0.5 * r15 * (ux * ux - uy * uy),
        ]
        for i in range(8):
            harm[i : i + 1, sl] = hs[i]
        k = (lax.broadcasted_iota(jnp.int32, (8, block), 0) + 1).astype(F32)
        t = k * ratio
        n = jnp.floor(t + 0.5)
        r = t - n
        sgn = 1.0 - 2.0 * (n - 2.0 * jnp.floor(n * 0.5))
        q = r * r
        s_pi = pi**9 / 362880.0 - q * (pi**11 / 39916800.0)
        s_pi = pi**7 / 5040.0 - q * s_pi
        s_pi = pi**5 / 120.0 - q * s_pi
        s_pi = pi**3 / 6.0 - q * s_pi
        s_pi = r * (pi - q * s_pi)
        c_pi = pi**10 / 3628800.0 - q * (pi**12 / 479001600.0)
        c_pi = pi**8 / 40320.0 - q * c_pi
        c_pi = pi**6 / 720.0 - q * c_pi
        c_pi = pi**4 / 24.0 - q * c_pi
        c_pi = pi**2 / 2.0 - q * c_pi
        c_pi = 1.0 - q * c_pi
        amp = sgn * (inv * env)
        bas = s_pi * amp
        dbasis[:, sl] = c_pi * amp * (k * (pi / 5.0)) - bas * (inv + (6.0 / 5.0) * (env * ra5))
        bh = bas.astype(BF16).astype(F32)
        bl = bas - bh
        basis2[:, sl] = jnp.concatenate([bh, bl], axis=0).astype(BF16)
        bstack = jnp.concatenate([bh, bl, bh, jnp.zeros_like(bh)], axis=0).astype(BF16)
        pre = mm(w1_t, bstack)
        spot = lax.broadcasted_iota(jnp.int32, (1, block), 1)
        live = jnp.where(spot < live_count, 1.0, 0.0)
        sig = 1.0 / (1.0 + jnp.exp(-pre))
        sig_live = sig * live
        hid = pre * sig_live
        dsilu[:, sl] = sig_live * (1.0 + pre * (1.0 - sig))
        hh, hl = split(hid)
        hidden[:, sl] = hh
        radial[:, sl] = mm(w2_t, jnp.concatenate([hh, hl, hh], axis=0))

        for deg, ms in enumerate(((0,), (1, 2, 3), (4, 5, 6, 7, 8))):
            total = None
            for m in ms:
                term = dall[m * width : (m + 1) * width]
                if m > 0:
                    term = term * hs[m - 1]
                total = term if total is None else total + term
            dweight[deg * width : (deg + 1) * width, sl] = total

    part_one(edges)

    for copy in ghosts:
        if comm:
            copy.wait_recv()
        else:
            copy.wait()
    table_t = jnp.concatenate(
        [table[c * CHUNK : (c + 1) * CHUNK, :].T for c in range(chunks)], axis=0
    )

    def gather(b):
        sl = pl.ds(pl.multiple_of(b * block, block), block)
        chunk = part[:, sl]
        got = mm(table_t, one_src[:, sl])
        g = got[0:width]
        for c in range(1, chunks):
            g = jnp.where(chunk == c, got[c * width : (c + 1) * width], g)
        gathered[:, sl] = g

    def part_two(b, carry):
        sl = pl.ds(pl.multiple_of(b * block, block), block)
        gather(b)
        g = gathered[:, sl]
        drad = jnp.concatenate(
            [(dweight[deg * width : (deg + 1) * width, sl] * g).astype(BF16) for deg in range(3)], axis=0
        )
        weighted = [radial[deg * width : (deg + 1) * width, sl] * g for deg in range(3)]
        halves = [w.astype(BF16) for w in weighted]
        terms = [halves[0]]
        for m in range(1, 9):
            terms.append(halves[DEGREE[m]] * harm[m - 1 : m, sl].astype(BF16))
        dhid = mm(w2_both, drad)
        dw_two[...] += mm_nt(hidden[:, sl], drad)
        acc[...] += (mm_nt(jnp.concatenate(terms, axis=0), one_dst[:, sl]))
        dpre[:, sl] = ((dhid[:64] + dhid[64:]) * dsilu[:, sl]).astype(BF16)
        return carry

    lax.fori_loop(0, edges // block, part_two, 0)
    dw_one = mm_nt(basis2[...], dpre[...])

    accb = [(acc[m * width : (m + 1) * width, :] * factor).astype(BF16) for m in range(9)]
    for deg in range(3):
        total = None
        for m in range(9):
            if DEGREE[m] == deg:
                one = mm(accb[m], cot[:, m * width : (m + 1) * width])
                total = one if total is None else total + one
        ar_half[deg * width : (deg + 1) * width, :] = total.astype(BF16)
    row = 3 * width
    for deg in range(3):
        ar_half[row : row + 64, :] = dw_two[:, deg * width : (deg + 1) * width].astype(BF16)
        row += 64
    tail = jnp.concatenate([dw_one[0:8, :] + dw_one[8:16, :], jnp.zeros((8, 64), F32)], axis=0)
    tail = jnp.concatenate([tail, jnp.zeros((16, 64), F32)], axis=1)
    ar_half[row : row + 16, :] = tail.astype(BF16)
    ar_half[row + 16 :, :] = jnp.zeros((ar_half.shape[0] - row - 16, width), BF16)

    def rows_of(q):
        return pl.ds(pl.multiple_of(q * SLICE, SLICE), SLICE)

    def copy_one(u, q):
        slot = lax.rem(member - u + group, group)
        return remote(in_plane(u), ar_half.at[rows_of(q)], got_one.at[slot], one_send, one_recv)

    def copy_two(s):
        return remote(along(s * PLANE_X), got_two.at[plane], got_two.at[plane], two_send, two_recv)

    def copy_three(u):
        return remote(in_plane(u), half_three, final.at[rows_of(my_slice)], three_send, three_recv)

    here = {"gx": me_x, "gy": me_y}
    all_one = remote(here, got_one.at[pl.ds(1, group - 1)], got_one.at[pl.ds(1, group - 1)], one_send, one_recv)
    all_two = remote(here, got_two.at[pl.ds(1, planes - 1)], got_two.at[pl.ds(1, planes - 1)], two_send, two_recv)
    most = pl.ds(0, (SLICES - 1) * SLICE)
    all_rows = remote(here, ar_half, final, one_send, three_recv)
    most_rows = remote(here, ar_half.at[most], final.at[most], one_send, three_recv)

    if comm:

        def send_one(u):
            q = lax.rem(u * SPREAD_INVERSE, group)

            @pl.when(q < SLICES)
            def _():
                copy_one(u, q).start()

        plane_loop(send_one, FAR_FIRST)

    def scatter(b, carry):
        sl = pl.ds(pl.multiple_of(b * block, block), block)
        chunk = part[:, sl]
        dg = None
        for deg in range(3):
            rws = slice(deg * width, (deg + 1) * width)
            one = radial[rws, sl] * dweight[rws, sl]
            dg = one if dg is None else dg + one
        dgm = jnp.concatenate([jnp.where(chunk == c, dg, 0.0).astype(BF16) for c in range(chunks)], axis=0)
        dtab[...] += mm_nt(one_src[:, sl], dgm)
        return carry

    lax.fori_loop(0, edges // block, scatter, 0)

    for c in range(chunks):
        dtab_out[c * CHUNK : (c + 1) * CHUNK, :] = dtab[:, c * width : (c + 1) * width].astype(BF16)
    returns = [
        to_peer(
            p,
            dtab_out.at[pl.ds(owned + p * slots, slots)],
            back.at[pl.ds(p * slots, slots)],
            back_send,
            back_recv,
            -1,
        )
        for p in range(6)
    ]
    for copy in returns:
        copy.start()

    if comm:

        @pl.when(owner)
        def _():
            all_one.wait_recv()
            total = ar_half[rows_of(my_slice), :].astype(F32)
            for s in range(1, group):
                total = total + got_one[s].astype(F32)
            got_two[plane] = total.astype(BF16)
            loop(1, planes, lambda s: copy_two(s).start())

    def sums(b, carry):
        sl = pl.ds(pl.multiple_of(b * 256, 256), 256)
        for deg in range(3):
            w = radial[deg * width : (deg + 1) * width, sl] * gathered[:, sl]
            for m in range(1, 9):
                if DEGREE[m] == deg:
                    d = dterms[m * width : (m + 1) * width, sl].astype(F32)
                    dharm[m - 1 : m, sl] = jnp.sum(w * d, axis=0, keepdims=True)
        return carry

    lax.fori_loop(0, edges // 256, sums, 0, unroll=2)

    if comm:

        @pl.when(owner)
        def _():
            all_two.wait_recv()
            total = got_two[0].astype(F32)
            for s in range(1, planes):
                total = total + got_two[s].astype(F32)
            half_three[...] = total.astype(BF16)
            plane_loop(lambda u: copy_three(u).start(), FAR_FIRST)
            own = pltpu.make_async_copy(half_three, final.at[rows_of(my_slice)], own_sem)
            own.start()
            own.wait()

    dbas = mm(w1_both, dpre[...])
    ddist = jnp.sum((dbas[:8] + dbas[8:]) * dbasis[...], axis=0, keepdims=True)
    ux, uy, uz, inv = (geom[i : i + 1, :] for i in range(4))
    g1, g2, g3, g4, g5, g6, g7, g8 = (dharm[i : i + 1, :] for i in range(8))
    dx = r3 * g1 + r15 * (g4 * uy + g7 * uz + g8 * ux)
    dy = r3 * g2 + r15 * (g4 * ux + g5 * uz - g8 * uy)
    dz = r3 * g3 + r15 * (g5 * uy + g7 * ux) + (3.0 * r5) * (uz * g6)
    dd = ddist - (dx * ux + dy * uy + dz * uz) * inv
    force[0:1, :] = dx * inv + ux * dd
    force[1:2, :] = dy * inv + uy * dd
    force[2:3, :] = dz * inv + uz * dd

    for deg in range(3):
        hi, lo = mix_hl[deg]
        mix_t = jnp.concatenate([mm_nt(eye128, hi), mm_nt(eye128, lo)], axis=1).astype(BF16)
        for m in range(9):
            if DEGREE[m] == deg:
                out_t = mm(mix_t, jnp.concatenate([accb[m], accb[m]], axis=0)).astype(BF16)
                mixed[:, m * width : (m + 1) * width] = out_t.T
    stores = [
        pltpu.make_async_copy(a, b, out_sem.at[i])
        for i, (a, b) in enumerate(((mixed, mixed_far), (grad_feat, grad_feat_far), (force, force_far)))
    ]
    stores[0].start()
    stores[2].start()

    for copy in returns:
        if comm:
            copy.wait_recv()
        else:
            copy.wait()
    total = dtab[:, 0:width]
    for p in range(6):
        total = total + mm(picks(p), back[p * slots : (p + 1) * slots, :])
    grad_feat[...] = total
    stores[1].start()

    if comm:
        for copy in ghosts:
            copy.wait_send()
        for copy in returns:
            copy.wait_send()

        @pl.when(owner)
        def _():
            most_rows.wait_send()
            all_two.wait_send()
            loop(1, group, lambda s: copy_three(member).wait_send())
            most_rows.wait_recv()

        @pl.when(jnp.logical_not(owner))
        def _():
            all_rows.wait_send()
            all_rows.wait_recv()

    else:
        own = pltpu.make_async_copy(ar_half, final, own_sem)
        own.start()
        own.wait()
    for store in stores:
        store.wait()


def finish(*refs):
    inputs, outputs = refs[:4], refs[4:10]
    near, grads, in_sem, out_sem = refs[10:14], refs[14:17], refs[17], refs[18]
    loads = [pltpu.make_async_copy(a, b, in_sem.at[i]) for i, (a, b) in enumerate(zip(inputs, near))]
    stores = [
        pltpu.make_async_copy(a, b, out_sem.at[i])
        for i, (a, b) in enumerate(zip((*near[:3], *grads), outputs))
    ]
    for i in (3, 0, 1, 2):
        loads[i].start()
    rows = near[3]
    grad_one, grad_two, grad_mix = grads
    width = rows.shape[1]
    loads[3].wait()
    for deg in range(3):
        grad_mix[deg] = rows[deg * width : (deg + 1) * width, :].astype(F32)
    stores[5].start()
    row = 3 * width
    for deg in range(3):
        grad_two[:, deg * width : (deg + 1) * width] = rows[row : row + 64, :].astype(F32)
        row += 64
    stores[4].start()
    grad_one[...] = rows[row : row + 16, :].astype(F32)[0:8, 0:64]
    stores[3].start()
    for i in (0, 1, 2):
        loads[i].wait()
        stores[i].start()
    for store in stores:
        store.wait()


def on_device(
    nx,
    ny,
    block,
    features,
    edge_vec,
    edge_src,
    edge_dst,
    edge_count,
    send_gx,
    send_gy,
    w_one,
    w_two,
    mix,
    cotangent,
):
    owned, width = features.shape
    edges = edge_vec.shape[1]
    slots = send_gx.shape[1]
    hid = w_one.shape[1]
    rows = -(-(owned + 6 * slots) // CHUNK) * CHUNK
    chunks = rows // CHUNK
    group = PLANE_X * ny
    planes = max(nx // PLANE_X, 2)
    vmem = pl.BlockSpec(memory_space=pltpu.VMEM)
    far = pl.BlockSpec(memory_space=pl.ANY)
    dma = pltpu.SemaphoreType.DMA
    args = (
        features,
        edge_vec,
        edge_src.reshape(1, edges),
        edge_dst.reshape(1, edges),
        edge_count.reshape(1, 1),
        send_gx,
        send_gy,
        w_one,
        w_two,
        mix,
        cotangent,
    )
    shapes = (
        jax.ShapeDtypeStruct((owned, 9 * width), BF16),
        jax.ShapeDtypeStruct((owned, width), F32),
        jax.ShapeDtypeStruct((3, edges), F32),
    )
    scratch = [
        *(pltpu.VMEM(a.shape, a.dtype) for a in args),
        *(pltpu.VMEM(a.shape, a.dtype) for a in shapes),
        pltpu.VMEM((rows, width), BF16),
        pltpu.VMEM((6 * slots, width), BF16),
        pltpu.VMEM((rows, width), BF16),
        pltpu.VMEM((6 * slots, width), BF16),
        pltpu.VMEM((CHUNK, chunks * width), F32),
        pltpu.VMEM((9 * width, owned), F32),
        pltpu.VMEM((9 * width, owned), BF16),
        pltpu.VMEM((CHUNK, edges), BF16),
        pltpu.VMEM((owned, edges), BF16),
        pltpu.VMEM((3 * width, edges), F32),
        pltpu.VMEM((3 * width, edges), F32),
        pltpu.VMEM((9 * width, edges), BF16),
        pltpu.VMEM((hid, edges), F32),
        pltpu.VMEM((hid, edges), BF16),
        pltpu.VMEM((8, edges), F32),
        pltpu.VMEM((16, edges), BF16),
        pltpu.VMEM((8, edges), F32),
        pltpu.VMEM((8, edges), F32),
        pltpu.VMEM((1, edges), jnp.int32),
        pltpu.VMEM((8, edges), F32),
        pltpu.VMEM((hid, 3 * width), F32),
        pltpu.VMEM((hid, edges), BF16),
        pltpu.VMEM((width, edges), F32),
        pltpu.VMEM((SLICES * SLICE, width), BF16),
        pltpu.VMEM((group, SLICE, width), BF16),
        pltpu.VMEM((planes, SLICE, width), BF16),
        pltpu.VMEM((SLICE, width), BF16),
        dma((6,)),
        dma((6,)),
        dma((6,)),
        dma((6,)),
        dma,
        dma,
        dma,
        dma,
        dma,
        dma,
        dma,
        dma((11,)),
        dma((3,)),
    ]
    params = {"vmem_limit_bytes": 60 * 1024 * 1024}
    if nx > 1:
        params.update(collective_id=0, has_side_effects=True)
    mixed, grad_feat, force, final = pl.pallas_call(
        functools.partial(kernel, nx, ny, block),
        out_shape=(*shapes, jax.ShapeDtypeStruct((SLICES * SLICE, width), BF16)),
        in_specs=[far] * 11,
        out_specs=(far,) * 4,
        scratch_shapes=scratch,
        compiler_params=pltpu.CompilerParams(**params),
        name="interaction",
    )(*args)
    grads = tuple(jax.ShapeDtypeStruct(w.shape, F32) for w in (w_one, w_two, mix))
    return pl.pallas_call(
        finish,
        out_shape=(*shapes, *grads),
        in_specs=[far] * 4,
        out_specs=(far,) * 6,
        scratch_shapes=[
            *(pltpu.VMEM(a.shape, a.dtype) for a in (*shapes, final, *grads)),
            dma((4,)),
            dma((6,)),
        ],
        name="finish",
    )(mixed, grad_feat, force, final)


def solution(mesh, block=2048):
    tiles = ("gx", "gy")
    return jax.shard_map(
        functools.partial(on_device, mesh.shape["gx"], mesh.shape["gy"], block),
        mesh=mesh,
        in_specs=(
            P(tiles, None),
            P(None, tiles),
            P(tiles),
            P(tiles),
            P(tiles),
            P(tiles, None),
            P(tiles, None),
            P(),
            P(),
            P(),
            P(tiles, None),
        ),
        out_specs=(
            P(tiles, None),
            P(tiles, None),
            P(None, tiles),
            P(),
            P(),
            P(),
        ),
        check_vma=False,
    )
```
